128 devices in a mesh: dp: 16 (over y, z), mp: 8 (over x, core).
Axes of the slice: x: 4, y: 4, z: 4, core: 2. Of those that a mesh axis runs over, the one named last changes fastest.
Arguments:
- joined_rows: bfloat16 [4096, 24576], P('dp', 'mp'), may hold values from -6 to 6
- fc_weight: bfloat16 [24576, 8192], P('mp', 'dp'), may hold values from -0.0390625 to 0.0390625
- target_features: bfloat16 [4096, 8192], P('mp', 'dp'), may hold values from -6 to 6
- segment_ids: int32 [4096], P('mp'), may hold values from 0 to 63, never falling along the last dimension, each value on 1 to 512 neighbouring positions
- step_gains: float32 [3, 8192], P(None, 'dp'), may hold values from 0.25 to 1.75
Outputs:
- mean_loss: float32 [], replicated
- grad_weight: float32 [24576, 8192], P('mp', 'dp')
The draws below stay inside these ranges and needn't reach their ends.
All inputs are finite; a program needn't handle non-finite values.
Results may differ from the reference program's by a relative error of at most 0.0029.
Values may be sent and summed in bfloat16 or wider, within the bound.
No kernel may reach another device: no remote copies, remote signals or barrier semaphores. Data moves between devices by JAX's collectives and lax.ppermute only.
A program may use at most 128 MiB of HBM per device.

```python
import math
import jax
import jax.numpy as jnp
import numpy as np
from jax import lax

D = 8192
F = 24576
STEPS = 3
TOKENS = 4096


def shard_levels(stream_key, dims, split, smallest, largest):
    level = 1.0
    for dim, blocks in split:
        steps = jax.random.uniform(jax.random.fold_in(jax.random.fold_in(stream_key, 6), dim), (blocks,), jnp.float32, smallest / len(split), largest / len(split))
        level = level * jnp.repeat(jnp.exp(steps), dims[dim] // blocks).reshape((-1,) + (1,) * (len(dims) - 1 - dim))
    return level


def split_up(number_of, total, limit, skew):
    portions = [(1 << 20) // math.isqrt(rank ** skew) + 1 for rank in range(2, number_of + 1)]
    surplus, holding = total - limit - (number_of - 1), [1] * (number_of - 1)
    while surplus > 0:
        free = [i for i in range(number_of - 1) if holding[i] < limit]
        pool, remaining = sum([portions[i] for i in free]), surplus
        for i in free:
            extra = min(limit - holding[i], max(1, remaining * portions[i] // pool), surplus)
            holding[i] = holding[i] + extra
            surplus = surplus - extra
    return np.array([limit] + holding)


def ragged_sizes(stream_key, amount, total, reach, skew):
    if amount == 2:
        one = jax.random.randint(stream_key, (), max(1, total - reach), min(reach, total - 1) + 1)
        return jnp.stack([one, total - one])
    lengths = jnp.asarray(split_up(amount, total, reach, skew), jnp.int32)
    couples = (amount - 1) // 2
    donor, taker = lengths[1:1 + 2 * couples:2], lengths[2:2 + 2 * couples:2]
    slack = jnp.minimum(donor - 1, reach - taker)
    moved = jax.random.randint(jax.random.fold_in(stream_key, 1), (couples,), 0, 1 << 20) % (slack + 1)
    lengths = lengths.at[1:1 + 2 * couples:2].set(donor - moved).at[2:2 + 2 * couples:2].set(taker + moved)
    return lengths[jax.random.permutation(jax.random.fold_in(stream_key, 2), amount)]


def gaussian(key, dims, deviation, limit, split=(), dtype=jnp.bfloat16):
    result = jax.random.normal(key, dims, jnp.float32) * deviation
    if len(split) > 0:
        result = shard_levels(key, dims, split, -0.22, 0.18) * result
    return jnp.clip(result, min=-limit, max=limit).astype(dtype)


def setup_inputs(seed: int = 0) -> dict:
    key_list = jax.random.split(jax.random.key(seed), 6)
    return {
        "joined_rows": gaussian(key_list[0], (TOKENS, F), 1.0, 6.0, ((0, 16), (1, 8))),
        "fc_weight": gaussian(key_list[1], (F, D), F ** -0.5, 0.0390625, ((0, 8), (1, 16))),
        "target_features": gaussian(key_list[2], (TOKENS, D), 1.0, 6.0, ((0, 8), (1, 16))),
        "segment_ids": jnp.searchsorted(jnp.cumsum(ragged_sizes(key_list[3], max(TOKENS // 64, 4), TOKENS, min(TOKENS // 2, 512), 2)), jnp.arange(TOKENS), side="right").astype(jnp.int32),
        "step_gains": jnp.clip(1.0 + 0.15 * jax.random.normal(key_list[4], (STEPS, D), jnp.float32), 0.25, 1.75),
    }


EPSILON = 1e-06

def reference(joined_rows, fc_weight, target_features, segment_ids, step_gains):
    total_rows = joined_rows.shape[0]
    first_state = jnp.dot(joined_rows, fc_weight, preferred_element_type=jnp.float32)
    segments = segment_ids.astype(jnp.int32)
    prev_keep = jnp.concatenate([jnp.zeros((1,), jnp.bool_), segments[1:] == segments[:-1]]).astype(jnp.float32)
    targets = target_features.astype(jnp.float32)

    def unroll(start_state):
        draft_state = start_state
        err_total = jnp.zeros((), jnp.float32)
        count_total = jnp.zeros((), jnp.float32)
        for step_index in range(STEPS):
            shifted = jnp.concatenate([jnp.zeros((1, D), jnp.float32), draft_state[:-1]], axis=0) * prev_keep[:, None]
            mixed_rows = start_state + shifted
            scale_rows = lax.rsqrt(lax.optimization_barrier(jnp.mean(mixed_rows * mixed_rows, axis=1, keepdims=True)) + EPSILON)
            draft_state = mixed_rows * scale_rows * step_gains[step_index]
            goal_rows = jnp.concatenate([targets[step_index:], jnp.zeros((step_index, D), jnp.float32)], axis=0)
            later_ids = jnp.concatenate([segments[step_index:], jnp.full((step_index,), -1, jnp.int32)])
            kept_mask = (later_ids == segments).astype(jnp.float32)
            error_rows = (draft_state - goal_rows) * kept_mask[:, None]
            err_total = err_total + jnp.sum(error_rows * error_rows)
            count_total = count_total + jnp.sum(kept_mask)
        return (err_total, count_total)
    (err_total, count_total), pullback = jax.vjp(unroll, first_state)
    pull_seed = jnp.asarray(0.5 / math.sqrt(total_rows), jnp.float32)
    grad_state, = pullback((pull_seed, jnp.zeros((), jnp.float32)))
    grad_rows = grad_state.astype(jnp.bfloat16)
    grad_weight = jnp.dot(joined_rows.T, grad_rows, preferred_element_type=jnp.float32)
    mean_loss = err_total / (2.0 * D * count_total)
    return (mean_loss, grad_weight)
```

```python
import math

import jax
import jax.numpy as jnp
from jax import lax
from jax.experimental import pallas as pl
from jax.experimental.pallas import tpu as pltpu
from jax.sharding import PartitionSpec as P

D = 8192
STEPS = 3
EPSILON = 1e-06

PAD = 16
LANES = 640
PRODUCTS = 24
VMEM = 48 * 1024 * 1024


def along_dp(block, dy, dz):
    route = [
        (y * 4 + z, (y + dy) % 4 * 4 + (z + dz) % 4) for y in range(4) for z in range(4)
    ]
    return lax.ppermute(block, "dp", route)


def along_mp(block, dx, dcore):
    route = [(x * 2 + c, (x + dx) % 4 * 2 + (c ^ dcore)) for x in range(4) for c in range(2)]
    return lax.ppermute(block, "mp", route)


def neighbour(block, distance):
    devices = range(lax.axis_size("mp"))
    route = [(i - distance, i) for i in devices if i - distance in devices]
    return lax.ppermute(block, "mp", route)


def down(block):
    return jnp.concatenate([block[-1:], block[:-1]], axis=0)


def up(block):
    return jnp.concatenate([block[1:], block[:1]], axis=0)


def before(row):
    return jnp.concatenate([row[:, -1:], row[:, :-1]], axis=1)


def after(row):
    return jnp.concatenate([row[:, 1:], row[:, :1]], axis=1)


def product_kernel(rows, state_ref, target_ref, keep_ref, gain_ref, out_ref, columns):
    gain0, gain1, gain2 = (gain_ref[k : k + 1, :] for k in range(STEPS))
    columns[...] = jnp.zeros_like(columns)
    lane = lax.broadcasted_iota(jnp.int32, (rows, 128), 1)

    def block(index, carry):
        start = pl.multiple_of(index * rows, 8)
        window = pl.ds(start, rows + 16)
        state, target, keep = state_ref[window, :], target_ref[window, :], keep_ref[window, :]
        previous = down(state)
        mixed0 = state + keep * previous
        scaled0 = gain0 * down(mixed0)
        second = gain1 * previous
        third = gain1 * down(scaled0)
        target1 = up(target)
        target2 = gain2 * up(target1)
        weight = gain2 * gain2
        weighted, weighted2, weighted3 = weight * state, weight * second, weight * third
        pairs = [
            (mixed0, mixed0),
            (state, state),
            (state, scaled0),
            (scaled0, scaled0),
            (state, second),
            (state, third),
            (second, second),
            (second, third),
            (third, third),
            (weighted, state),
            (weighted, second),
            (weighted, third),
            (weighted2, second),
            (weighted2, third),
            (weighted3, third),
            (target2, state),
            (target2, second),
            (target2, third),
            (gain1 * target1, state),
            (gain1 * target1, scaled0),
            (gain0 * target, mixed0),
        ]
        total = jnp.zeros((rows, 128), jnp.float32)
        for k, (left, right) in enumerate(pairs):
            value = jnp.sum((left * right)[8 : rows + 8], axis=1, keepdims=True)
            total = jnp.where(lane == k, value, total)
        columns[pl.ds(pl.multiple_of(start + 8, 8), rows), :] = total
        return carry

    lax.fori_loop(0, (state_ref.shape[0] - 16) // rows, block, 0)
    out_ref[...] = columns[...].T[:PRODUCTS, :]


def products(state, target, keep, gains):
    rows = 48
    return pl.pallas_call(
        lambda *refs: product_kernel(rows, *refs),
        out_shape=jax.ShapeDtypeStruct((PRODUCTS, LANES), jnp.float32),
        in_specs=[pl.BlockSpec(memory_space=pltpu.VMEM)] * 4,
        out_specs=pl.BlockSpec(memory_space=pltpu.VMEM),
        scratch_shapes=[pltpu.VMEM((LANES, 128), jnp.float32)],
        compiler_params=pltpu.CompilerParams(vmem_limit_bytes=VMEM),
    )(state, target, keep, gains)


def coefficients(product, keep, factor):
    p = [None] + [product[k : k + 1, :] for k in range(21)]

    def scale(squares):
        return lax.rsqrt(jnp.maximum(squares, 0.0) / D + EPSILON)

    scale0 = scale(p[1])
    r0 = keep * before(scale0)
    scale1 = scale(p[2] + 2.0 * r0 * p[3] + r0 * r0 * p[4])
    a = keep * before(scale1)
    b = a * before(r0)
    scale2 = scale(
        p[2] + a * a * p[7] + b * b * p[9] + 2.0 * a * p[5] + 2.0 * b * p[6] + 2.0 * a * b * p[8]
    )
    same_next = after(keep)
    same_second = same_next * after(same_next)
    x1 = p[10] + a * p[11] + b * p[12]
    x2 = p[11] + a * p[13] + b * p[14]
    x3 = p[12] + a * p[14] + b * p[15]
    product2 = (
        factor
        * same_second
        * scale2
        * (scale2 * (x1 + a * x2 + b * x3) - (p[16] + a * p[17] + b * p[18]))
    )
    alpha2 = factor * same_second * scale2 * scale2
    gamma2 = -factor * same_second * scale2
    beta2 = -scale2 * scale2 * product2 / D
    second = alpha2 * x2 + beta2 * (p[5] + a * p[7] + b * p[8]) + gamma2 * p[17]
    third = alpha2 * x3 + beta2 * (p[6] + a * p[8] + b * p[9]) + gamma2 * p[18]
    next7, next8, next9 = after(p[7]), after(p[8]), after(p[9])
    y1 = next7 + r0 * next8
    y2 = next8 + r0 * next9
    product1 = scale1 * (
        factor * same_next * (scale1 * (y1 + r0 * y2) - (p[19] + r0 * p[20]))
        + same_next * (after(second) + r0 * after(third))
    )
    alpha1 = factor * same_next * scale1 * scale1
    gamma1 = -factor * same_next * scale1
    eta1 = scale1 * same_next
    beta1 = -scale1 * scale1 * product1 / D
    carried = alpha1 * y2 + gamma1 * p[20] + eta1 * after(third) + beta1 * (p[3] + r0 * p[4])
    product0 = scale0 * (
        factor * (scale0 * after(p[4]) - p[21]) + same_next * after(carried)
    )
    alpha0 = factor * scale0 * scale0
    gamma0 = -factor * scale0
    eta0 = scale0 * same_next
    beta0 = -scale0 * scale0 * product0 / D
    return [
        r0, a, b, scale0, scale1, scale2, same_next, same_second,
        alpha2, beta2, gamma2, alpha1, beta1, gamma1, eta1, alpha0, beta0, gamma0, eta0,
    ]


def gradient_kernel(
    rows, factor, state_ref, target_ref, keep_ref, keep_row_ref, gain_ref, product_ref,
    grad_ref, error_ref, table, columns,
):
    gain0, gain1, gain2 = (gain_ref[k : k + 1, :] for k in range(STEPS))
    table[...] = jnp.zeros_like(table)
    found = coefficients(product_ref[...], keep_row_ref[...], factor)
    for k, row in enumerate(found):
        table[k : k + 1, :] = row
    columns[...] = table[...].T

    def block(index, carry):
        start = pl.multiple_of(index * rows + PAD - 8, 8)
        window = pl.ds(start, rows + 16)
        state, target, keep = state_ref[window, :], target_ref[window, :], keep_ref[window, :]
        values = columns[window, :]
        (
            r0, a, b, scale0, scale1, scale2, same_next, same_second,
            alpha2, beta2, gamma2, alpha1, beta1, gamma1, eta1, alpha0, beta0, gamma0, eta0,
        ) = (values[:, k : k + 1] for k in range(len(found)))
        previous = down(state)
        mixed0 = state + keep * previous
        scaled0 = gain0 * down(mixed0)
        mixed1 = state + r0 * scaled0
        mixed2 = state + gain1 * (a * previous + b * down(scaled0))
        target1 = up(target)
        target2 = up(target1)
        grad2 = (alpha2 * (gain2 * gain2) + beta2) * mixed2 + gamma2 * (gain2 * target2)
        grad1 = (alpha1 * (gain1 * gain1) + beta1) * mixed1 + gain1 * (
            gamma1 * target1 + eta1 * up(grad2)
        )
        grad0 = (alpha0 * (gain0 * gain0) + beta0) * mixed0 + gain0 * (
            gamma0 * target + eta0 * up(grad1)
        )
        grad = grad0 + grad1 + grad2 + same_next * up(grad0)
        grad_ref[pl.ds(pl.multiple_of(index * rows, 16), rows), :] = grad[8 : rows + 8].astype(
            jnp.bfloat16
        )
        error0 = scale0 * gain0 * mixed0 - target
        error1 = same_next * (scale1 * gain1 * mixed1 - target1)
        error2 = same_second * (scale2 * gain2 * mixed2 - target2)
        squares = (error0 * error0 + error1 * error1 + error2 * error2)[8 : rows + 8]
        count = (1.0 + same_next + same_second)[8 : rows + 8]
        return carry[0] + jnp.sum(squares, axis=0, keepdims=True), carry[1] + jnp.sum(
            count, axis=0, keepdims=True
        )

    zero = jnp.zeros((1, state_ref.shape[1]), jnp.float32)
    squares, count = lax.fori_loop(
        0, grad_ref.shape[0] // rows, block, (zero, jnp.zeros((1, 1), jnp.float32))
    )
    error = jnp.sum(squares, axis=1, keepdims=True)
    lane = lax.broadcasted_iota(jnp.int32, (1, 128), 1)
    error_ref[...] = jnp.where(lane == 0, error, jnp.where(lane == 1, count, 0.0))


def gradients(state, target, keep, keep_row, gains, product, factor):
    rows = 64
    own = state.shape[0] - 2 * PAD
    return pl.pallas_call(
        lambda *refs: gradient_kernel(rows, factor, *refs),
        out_shape=(
            jax.ShapeDtypeStruct((own, state.shape[1]), jnp.bfloat16),
            jax.ShapeDtypeStruct((1, 128), jnp.float32),
        ),
        in_specs=[pl.BlockSpec(memory_space=pltpu.VMEM)] * 6,
        out_specs=(pl.BlockSpec(memory_space=pltpu.VMEM),) * 2,
        scratch_shapes=[
            pltpu.VMEM((128, LANES), jnp.float32),
            pltpu.VMEM((LANES, 128), jnp.float32),
        ],
        compiler_params=pltpu.CompilerParams(vmem_limit_bytes=VMEM),
    )(state, target, keep, keep_row, gains, product)


def weight_kernel(place_ref, rows_ref, *refs):
    grads, out_ref = refs[:-1], refs[-1]
    total = None
    for k, grad_ref in enumerate(grads):
        size = grad_ref.shape[0]
        rows = rows_ref[pl.ds(pl.multiple_of(place_ref[k] * size, size), size), :]
        term = lax.dot_general(
            rows, grad_ref[...], (((0,), (0,)), ((), ())), preferred_element_type=jnp.float32
        )
        total = term if total is None else total + term
    out_ref[...] = total


def weight_gradient(rows, grads, places):
    tokens, features = rows.shape
    columns = grads[0].shape[1]
    width = 512
    return pl.pallas_call(
        weight_kernel,
        out_shape=jax.ShapeDtypeStruct((features, columns), jnp.float32),
        grid_spec=pltpu.PrefetchScalarGridSpec(
            num_scalar_prefetch=1,
            grid=(features // width,),
            in_specs=[pl.BlockSpec((tokens, width), lambda i, place: (0, i))]
            + [pl.BlockSpec(g.shape, lambda i, place: (0, 0)) for g in grads],
            out_specs=pl.BlockSpec((width, columns), lambda i, place: (i, 0)),
        ),
        compiler_params=pltpu.CompilerParams(vmem_limit_bytes=VMEM),
    )(places, rows, *grads)


def local(joined_rows, fc_weight, target_features, segment_ids, step_gains):
    mp_index = lax.axis_index("mp")
    x_index, core = mp_index // 2, mp_index % 2
    own = target_features.shape[0]
    columns = target_features.shape[1]
    gathered = lax.all_gather(joined_rows, "dp", axis=0, tiled=True)
    total_rows = gathered.shape[0]

    next_target = neighbour(target_features[:PAD], -1)
    segments = jnp.concatenate(
        [
            neighbour(segment_ids[-PAD - 1 :], 1),
            segment_ids,
            neighbour(segment_ids[:PAD], -1),
        ]
    )
    token = mp_index * own - PAD + jnp.arange(own + 2 * PAD, dtype=jnp.int32)
    keep = (
        (segments[1:] == segments[:-1]) & (token > 0) & (token < total_rows)
    ).astype(jnp.float32)
    keep_row = jnp.pad(keep, (0, LANES - keep.shape[0]))[None, :]
    keep = keep[:, None]
    target = jnp.concatenate(
        [jnp.zeros((PAD, columns), jnp.bfloat16), target_features, next_target]
    ).astype(jnp.float32)

    partial = jnp.dot(gathered, fc_weight, preferred_element_type=jnp.float32)
    partial = jnp.pad(partial, ((PAD, PAD), (0, 0)))

    def windows(which):
        return jnp.stack(
            [
                lax.dynamic_slice(
                    partial, ((2 * x + which) * own, 0), (own + 2 * PAD, columns)
                )
                for x in range(4)
            ]
        )

    summed = windows(core) + along_mp(windows(1 - core), 0, 1)
    state = lax.dynamic_index_in_dim(summed, x_index, 0, keepdims=False)
    for k in (1, 3, 2):
        block = lax.dynamic_index_in_dim(summed, (x_index + k) % 4, 0, keepdims=False)
        state = state + along_mp(block.astype(jnp.bfloat16), k, 0).astype(jnp.float32)

    product = products(state, target, keep, step_gains)
    product = product + sum(along_dp(product, 0, k) for k in (1, 2, 3))
    product = product + sum(along_dp(product, k, 0) for k in (1, 2, 3))
    factor = 1.0 / math.sqrt(total_rows)
    grad, error = gradients(state, target, keep, keep_row, step_gains, product, factor)

    sums = lax.all_gather(error, ("dp", "mp"), axis=0, tiled=True)
    grads = [grad] + [along_mp(grad, k, 0) for k in (1, 3, 2)]
    grads = grads + [along_mp(g, 0, 1) for g in grads]
    places = jnp.stack(
        [(x_index - k) % 4 * 2 + c for c in (core, 1 - core) for k in (0, 1, 3, 2)]
    ).astype(jnp.int32)
    grad_weight = weight_gradient(gathered, grads, places)
    error_total = jnp.sum(sums[:, 0])
    count_total = jnp.sum(sums[:, 1]) / lax.axis_size("dp")
    mean_loss = error_total / (2.0 * D * count_total)
    return (mean_loss, grad_weight)


def solution(mesh):
    in_specs = (P("dp", "mp"), P("mp", "dp"), P("mp", "dp"), P("mp"), P(None, "dp"))
    out_specs = (P(), P("mp", "dp"))
    return jax.shard_map(local, mesh=mesh, in_specs=in_specs, out_specs=out_specs, check_vma=False)
```

```python
import math

import jax
import jax.numpy as jnp
from jax import lax
from jax.experimental import pallas as pl
from jax.experimental.pallas import tpu as pltpu
from jax.sharding import PartitionSpec as P

D = 8192
STEPS = 3
EPSILON = 1e-06

SHARE = 32
PAD = 8
LENGTH = SHARE + 2 * PAD
BLOCKS = 16
PRODUCTS = 24
VMEM = 40 * 1024 * 1024


def from_dp(block, place):
    route = []
    for y in range(4):
        for z in range(4):
            sy, sz = place(y, z)
            route.append((sy % 4 * 4 + sz % 4, y * 4 + z))
    return lax.ppermute(block, "dp", route)


def along_mp(block, dx, dcore):
    route = [(x * 2 + c, (x + dx) % 4 * 2 + (c ^ dcore)) for x in range(4) for c in range(2)]
    return lax.ppermute(block, "mp", route)


def neighbour(block, distance):
    devices = range(lax.axis_size("mp"))
    route = [(i - distance, i) for i in devices if i - distance in devices]
    return lax.ppermute(block, "mp", route)


def down(block):
    return jnp.concatenate([block[-1:], block[:-1]], axis=0)


def up(block):
    return jnp.concatenate([block[1:], block[:1]], axis=0)


def before(row):
    return jnp.concatenate([row[:, -1:], row[:, :-1]], axis=1)


def after(row):
    return jnp.concatenate([row[:, 1:], row[:, :1]], axis=1)


def tie(value, *others):
    return lax.optimization_barrier((value, *others))[0]


FREE = pl.CostEstimate(flops=1, bytes_accessed=1, transcendentals=0)


def windows_kernel(block_rows, target_ref, out_ref):
    for owner in range(8):
        for block in range(2):
            start = block * block_rows + owner * SHARE + PAD
            out_ref[owner, block] = target_ref[start : start + LENGTH, :]


def windows(target, block_rows):
    return pl.pallas_call(
        lambda *refs: windows_kernel(block_rows, *refs),
        out_shape=jax.ShapeDtypeStruct((8, 2, LENGTH, target.shape[1]), target.dtype),
        in_specs=[pl.BlockSpec(memory_space=pltpu.VMEM)],
        out_specs=pl.BlockSpec(memory_space=pltpu.VMEM),
        compiler_params=pltpu.CompilerParams(vmem_limit_bytes=VMEM),
        cost_estimate=FREE,
        name="windows",
    )(target)


def product_kernel(state_ref, target_ref, keep_ref, gain_ref, out_ref, columns):
    gain0, gain1, gain2 = (gain_ref[k : k + 1, :] for k in range(STEPS))
    lane = lax.broadcasted_iota(jnp.int32, (LENGTH, 128), 1)

    def block(index, carry):
        state, target, keep = state_ref[index], target_ref[index], keep_ref[index]
        previous = down(state)
        mixed0 = state + keep * previous
        scaled0 = gain0 * down(mixed0)
        second = gain1 * previous
        third = gain1 * down(scaled0)
        target1 = up(target)
        target2 = gain2 * up(target1)
        weight = gain2 * gain2
        weighted, weighted2, weighted3 = weight * state, weight * second, weight * third
        pairs = [
            (mixed0, mixed0),
            (state, state),
            (state, scaled0),
            (scaled0, scaled0),
            (state, second),
            (state, third),
            (second, second),
            (second, third),
            (third, third),
            (weighted, state),
            (weighted, second),
            (weighted, third),
            (weighted2, second),
            (weighted2, third),
            (weighted3, third),
            (target2, state),
            (target2, second),
            (target2, third),
            (gain1 * target1, state),
            (gain1 * target1, scaled0),
            (gain0 * target, mixed0),
        ]
        total = jnp.zeros((LENGTH, 128), jnp.float32)
        for k, (left, right) in enumerate(pairs):
            value = jnp.sum(left * right, axis=1, keepdims=True)
            total = jnp.where(lane == k, value, total)
        columns[pl.ds(pl.multiple_of(index * LENGTH, 8), LENGTH), :] = total
        return carry

    lax.fori_loop(0, BLOCKS, block, 0)
    out_ref[...] = columns[...].T[:PRODUCTS, :]


def products(state, target, keep, gains):
    lanes = BLOCKS * LENGTH
    return pl.pallas_call(
        product_kernel,
        out_shape=jax.ShapeDtypeStruct((PRODUCTS, lanes), jnp.float32),
        in_specs=[pl.BlockSpec(memory_space=pltpu.VMEM)] * 4,
        out_specs=pl.BlockSpec(memory_space=pltpu.VMEM),
        scratch_shapes=[pltpu.VMEM((lanes, 128), jnp.float32)],
        compiler_params=pltpu.CompilerParams(vmem_limit_bytes=VMEM),
        cost_estimate=FREE,
        name="products",
    )(state, target, keep, gains)


def coefficients(product, keep, factor):
    p = [None] + [product[k : k + 1, :] for k in range(21)]

    def scale(squares):
        return lax.rsqrt(jnp.maximum(squares, 0.0) / D + EPSILON)

    scale0 = scale(p[1])
    r0 = keep * before(scale0)
    scale1 = scale(p[2] + 2.0 * r0 * p[3] + r0 * r0 * p[4])
    a = keep * before(scale1)
    b = a * before(r0)
    scale2 = scale(
        p[2] + a * a * p[7] + b * b * p[9] + 2.0 * a * p[5] + 2.0 * b * p[6] + 2.0 * a * b * p[8]
    )
    same_next = after(keep)
    same_second = same_next * after(same_next)
    x1 = p[10] + a * p[11] + b * p[12]
    x2 = p[11] + a * p[13] + b * p[14]
    x3 = p[12] + a * p[14] + b * p[15]
    product2 = (
        factor
        * same_second
        * scale2
        * (scale2 * (x1 + a * x2 + b * x3) - (p[16] + a * p[17] + b * p[18]))
    )
    alpha2 = factor * same_second * scale2 * scale2
    gamma2 = -factor * same_second * scale2
    beta2 = -scale2 * scale2 * product2 / D
    second = alpha2 * x2 + beta2 * (p[5] + a * p[7] + b * p[8]) + gamma2 * p[17]
    third = alpha2 * x3 + beta2 * (p[6] + a * p[8] + b * p[9]) + gamma2 * p[18]
    next7, next8, next9 = after(p[7]), after(p[8]), after(p[9])
    y1 = next7 + r0 * next8
    y2 = next8 + r0 * next9
    product1 = scale1 * (
        factor * same_next * (scale1 * (y1 + r0 * y2) - (p[19] + r0 * p[20]))
        + same_next * (after(second) + r0 * after(third))
    )
    alpha1 = factor * same_next * scale1 * scale1
    gamma1 = -factor * same_next * scale1
    eta1 = scale1 * same_next
    beta1 = -scale1 * scale1 * product1 / D
    carried = alpha1 * y2 + gamma1 * p[20] + eta1 * after(third) + beta1 * (p[3] + r0 * p[4])
    product0 = scale0 * (
        factor * (scale0 * after(p[4]) - p[21]) + same_next * after(carried)
    )
    alpha0 = factor * scale0 * scale0
    gamma0 = -factor * scale0
    eta0 = scale0 * same_next
    beta0 = -scale0 * scale0 * product0 / D
    return [
        r0, a, b, scale0, scale1, scale2, same_next, same_second,
        alpha2, beta2, gamma2, alpha1, beta1, gamma1, eta1, alpha0, beta0, gamma0, eta0,
    ]


def gradient_kernel(
    factor, state_ref, target_ref, keep_ref, keep_row_ref, gain_ref, product_ref,
    grad_ref, error_ref, table, columns,
):
    gain0, gain1, gain2 = (gain_ref[k : k + 1, :] for k in range(STEPS))
    table[...] = jnp.zeros_like(table)
    found = coefficients(product_ref[...], keep_row_ref[...], factor)
    for k, row in enumerate(found):
        table[k : k + 1, :] = row
    columns[...] = table[...].T

    def block(index, carry):
        state, target, keep = state_ref[index], target_ref[index], keep_ref[index]
        values = columns[pl.ds(pl.multiple_of(index * LENGTH, 8), LENGTH), :]
        (
            r0, a, b, scale0, scale1, scale2, same_next, same_second,
            alpha2, beta2, gamma2, alpha1, beta1, gamma1, eta1, alpha0, beta0, gamma0, eta0,
        ) = (values[:, k : k + 1] for k in range(len(found)))
        previous = down(state)
        mixed0 = state + keep * previous
        scaled0 = gain0 * down(mixed0)
        mixed1 = state + r0 * scaled0
        mixed2 = state + gain1 * (a * previous + b * down(scaled0))
        target1 = up(target)
        target2 = up(target1)
        grad2 = (alpha2 * (gain2 * gain2) + beta2) * mixed2 + gamma2 * (gain2 * target2)
        grad1 = (alpha1 * (gain1 * gain1) + beta1) * mixed1 + gain1 * (
            gamma1 * target1 + eta1 * up(grad2)
        )
        grad0 = (alpha0 * (gain0 * gain0) + beta0) * mixed0 + gain0 * (
            gamma0 * target + eta0 * up(grad1)
        )
        grad = grad0 + grad1 + grad2 + same_next * up(grad0)
        grad_ref[index] = grad[PAD : PAD + SHARE].astype(jnp.bfloat16)
        error0 = scale0 * gain0 * mixed0 - target
        error1 = same_next * (scale1 * gain1 * mixed1 - target1)
        error2 = same_second * (scale2 * gain2 * mixed2 - target2)
        squares = (error0 * error0 + error1 * error1 + error2 * error2)[PAD : PAD + SHARE]
        count = (1.0 + same_next + same_second)[PAD : PAD + SHARE]
        return carry[0] + jnp.sum(squares, axis=0, keepdims=True), carry[1] + jnp.sum(
            count, axis=0, keepdims=True
        )

    zero = jnp.zeros((1, state_ref.shape[2]), jnp.float32)
    squares, count = lax.fori_loop(
        0, BLOCKS, block, (zero, jnp.zeros((1, 1), jnp.float32))
    )
    error = jnp.sum(squares, axis=1, keepdims=True)
    lane = lax.broadcasted_iota(jnp.int32, (1, 128), 1)
    error_ref[...] = jnp.where(lane == 0, error, jnp.where(lane == 1, count, 0.0))


def gradients(state, target, keep, keep_row, gains, product, factor):
    lanes = product.shape[1]
    grad = jax.ShapeDtypeStruct((BLOCKS, SHARE, state.shape[2]), jnp.bfloat16)
    return pl.pallas_call(
        lambda *refs: gradient_kernel(factor, *refs),
        out_shape=(grad, jax.ShapeDtypeStruct((1, 128), jnp.float32)),
        in_specs=[pl.BlockSpec(memory_space=pltpu.VMEM)] * 6,
        out_specs=(pl.BlockSpec(memory_space=pltpu.VMEM),) * 2,
        scratch_shapes=[
            pltpu.VMEM((128, lanes), jnp.float32),
            pltpu.VMEM((lanes, 128), jnp.float32),
        ],
        compiler_params=pltpu.CompilerParams(vmem_limit_bytes=VMEM),
        cost_estimate=FREE,
        name="gradients",
    )(state, target, keep, keep_row, gains, product)


def project_kernel(pieces, blocks, core_ref, weight_ref, *refs):
    rows, (send_ref, keep_ref, total) = refs[:pieces], refs[pieces:]
    total[...] = jnp.dot(
        jnp.concatenate([r[...] for r in rows], axis=0),
        weight_ref[...],
        preferred_element_type=jnp.float32,
    )
    core = core_ref[0]
    for x in range(4):
        for block in range(blocks):
            start = (block * 4 + x) * 2 * SHARE
            keep = pl.ds(pl.multiple_of(start + core * SHARE, SHARE), SHARE)
            send = pl.ds(pl.multiple_of(start + (1 - core) * SHARE, SHARE), SHARE)
            keep_ref[x, block] = total[keep, :]
            send_ref[x, block] = total[send, :].astype(jnp.bfloat16)


def project(rows, weight, core):
    columns = weight.shape[1]
    tokens = sum(r.shape[0] for r in rows)
    blocks = tokens // (8 * SHARE)
    shape = (4, blocks, SHARE, columns)
    return pl.pallas_call(
        lambda *refs: project_kernel(len(rows), blocks, *refs),
        out_shape=(
            jax.ShapeDtypeStruct(shape, jnp.bfloat16),
            jax.ShapeDtypeStruct(shape, jnp.float32),
        ),
        in_specs=[pl.BlockSpec(memory_space=pltpu.SMEM)]
        + [pl.BlockSpec(memory_space=pltpu.VMEM)] * (len(rows) + 1),
        out_specs=(pl.BlockSpec(memory_space=pltpu.VMEM),) * 2,
        scratch_shapes=[pltpu.VMEM((tokens, columns), jnp.float32)],
        compiler_params=pltpu.CompilerParams(vmem_limit_bytes=VMEM),
        cost_estimate=FREE,
        name="project",
    )(jnp.stack([core]).astype(jnp.int32), weight, *rows)


def assemble_kernel(groups, place_ref, owner_ref, *refs):
    states, (before_ref, after_ref, window_ref) = refs[:groups], refs[groups:]
    first = (owner_ref[0] == 0).astype(jnp.int32)
    last = (owner_ref[0] == 7).astype(jnp.int32)
    edge = jnp.zeros((PAD, window_ref.shape[2]), jnp.float32)
    window_ref[0, :PAD] = edge
    window_ref[BLOCKS - 1, PAD + SHARE :] = edge
    k = 0
    for state_ref in states:
        for i in range(state_ref.shape[0]):
            block = place_ref[k]
            window_ref[block, PAD : PAD + SHARE] = state_ref[i]

            @pl.when(block + first < BLOCKS)
            def _():
                window_ref[jnp.minimum(block + first, BLOCKS - 1), :PAD] = before_ref[k]

            @pl.when(block >= last)
            def _():
                window_ref[jnp.maximum(block - last, 0), PAD + SHARE :] = after_ref[k]

            k += 1


def assemble(states, before, after, places, owner):
    return pl.pallas_call(
        lambda *refs: assemble_kernel(len(states), *refs),
        out_shape=jax.ShapeDtypeStruct((BLOCKS, LENGTH, before.shape[2]), jnp.float32),
        in_specs=[pl.BlockSpec(memory_space=pltpu.SMEM)] * 2
        + [pl.BlockSpec(memory_space=pltpu.VMEM)] * (len(states) + 2),
        out_specs=pl.BlockSpec(memory_space=pltpu.VMEM),
        compiler_params=pltpu.CompilerParams(vmem_limit_bytes=VMEM),
        cost_estimate=FREE,
        name="assemble",
    )(places, jnp.stack([owner]).astype(jnp.int32), *states, before, after)


def weight_kernel(pieces, block_ref, owner_ref, *refs):
    rows, grads, (out_ref, ordered) = refs[:pieces], refs[pieces : pieces + 2], refs[pieces + 2 :]

    @pl.when(pl.program_id(0) == 0)
    def _():
        for k in range(BLOCKS):
            for half in range(2):
                for i in range(4):
                    start = pl.multiple_of((k * 8 + owner_ref[half * 4 + i]) * SHARE, SHARE)
                    ordered[pl.ds(start, SHARE), :] = grads[half][i, block_ref[k]]

    out_ref[...] = lax.dot_general(
        jnp.concatenate([r[...] for r in rows], axis=0),
        ordered[...],
        (((0,), (0,)), ((), ())),
        preferred_element_type=jnp.float32,
    )


def weight_gradient(rows, blocks, mine, other, owners):
    features, columns = rows[0].shape[1], mine.shape[3]
    tokens = sum(r.shape[0] for r in rows)
    width = 512
    return pl.pallas_call(
        lambda *refs: weight_kernel(len(rows), *refs),
        out_shape=jax.ShapeDtypeStruct((features, columns), jnp.float32),
        grid_spec=pltpu.PrefetchScalarGridSpec(
            num_scalar_prefetch=2,
            grid=(features // width,),
            in_specs=[pl.BlockSpec((r.shape[0], width), lambda i, *_: (0, i)) for r in rows]
            + [pl.BlockSpec(mine.shape, lambda i, *_: (0, 0, 0, 0))] * 2,
            out_specs=pl.BlockSpec((width, columns), lambda i, *_: (i, 0)),
            scratch_shapes=[pltpu.VMEM((tokens, columns), jnp.bfloat16)],
        ),
        compiler_params=pltpu.CompilerParams(vmem_limit_bytes=VMEM),
        cost_estimate=FREE,
        name="weight_gradient",
    )(blocks, jnp.stack(owners).astype(jnp.int32), *rows, mine, other)


def sum_dp(value, places):
    return value + sum(from_dp(value, place) for place in places)


AROUND_Z = tuple(lambda y, z, k=k: (y, z + k) for k in (1, 3, 2))
AROUND_Y = tuple(lambda y, z, k=k: (y + k, z) for k in (1, 3, 2))


def step(block, dy, dz):
    return from_dp(block, lambda y, z: (y + dy, z + dz))


def ring(block, distance):
    return lax.ppermute(block, "mp", [((i - distance) % 8, i) for i in range(8)])


def local(joined_rows, fc_weight, target_features, segment_ids, step_gains):
    mp_index = lax.axis_index("mp")
    x_index, core = mp_index // 2, mp_index % 2
    dp_index = lax.axis_index("dp")
    y_index, z_index = dp_index // 4, dp_index % 4
    own, columns = target_features.shape
    block_rows = joined_rows.shape[0]
    total_rows = block_rows * lax.axis_size("dp")
    factor = 1.0 / math.sqrt(total_rows)
    barrier = lax.optimization_barrier

    def chip_sum(rows):
        send, kept = project(rows, fc_weight, core)
        return kept + along_mp(send, 0, 1).astype(jnp.float32)

    def first_state(summed):
        parts = [
            lax.dynamic_index_in_dim(summed, (x_index + k) % 4, 0, keepdims=False)
            for k in (0, 1, 3, 2)
        ]
        return parts[0] + sum(
            along_mp(part.astype(jnp.bfloat16), k, 0).astype(jnp.float32)
            for part, k in zip(parts[1:], (1, 3, 2))
        )

    own_block = joined_rows
    round1 = (
        step(own_block, 0, -1), step(own_block, 0, 1),
        step(own_block, -1, 0), step(own_block, 1, 0),
    )
    next_target = neighbour(target_features[: 2 * PAD], -1)
    next_segments = neighbour(segment_ids[: 2 * PAD], -1)
    last_segments = neighbour(segment_ids[-2 * PAD - 1 :], 1)
    round1, next_target, next_segments, last_segments = barrier(
        (round1, next_target, next_segments, last_segments)
    )
    b0m, b01, bm0, b10 = round1
    round2 = (step(b0m, -1, 0), step(bm0, 0, 1), step(b01, 1, 0), step(b10, 0, -1))

    segments = jnp.concatenate([last_segments, segment_ids, next_segments])
    token = mp_index * own - 2 * PAD + jnp.arange(own + 4 * PAD, dtype=jnp.int32)
    keep = (segments[1:] == segments[:-1]) & (token > 0) & (token < total_rows)
    target = jnp.concatenate(
        [jnp.zeros((2 * PAD, columns), jnp.bfloat16), target_features, next_target]
    )
    target = jnp.concatenate(
        [target, jnp.broadcast_to(keep.astype(jnp.bfloat16)[:, None], (target.shape[0], 128))],
        axis=1,
    )
    shares = lax.all_to_all(windows(target, block_rows), "mp", 0, 0, tiled=True)
    round2, shares = barrier((round2, shares))
    shares = shares.reshape(BLOCKS, LENGTH, columns + 128)
    target = shares[..., :columns].astype(jnp.float32)
    keep = shares[..., columns : columns + 1].astype(jnp.float32)
    keep_row = keep.reshape(1, BLOCKS * LENGTH)

    bmm, bm1, b11, b1m = round2
    round3 = (step(b0m, 0, -1), step(bm0, -1, 0), step(b11, 1, 0), step(b11, 0, 1))
    early = chip_sum([own_block, *round1, *round2])
    round3, early = barrier((round3, early))
    early = first_state(early)
    b02, b20, b21, b12 = round3
    half = block_rows // 2
    round4 = (
        step(bmm, 0, -1), step(bmm, -1, 0), step(b21[:half], 0, 1), step(b12[half:], 1, 0),
    )
    middle = chip_sum(round3)
    round4, early, middle = barrier((round4, early, middle))
    late = first_state(jnp.concatenate([middle, chip_sum(round4)], axis=1))

    names = [
        (0, 0), (0, -1), (0, 1), (-1, 0), (1, 0), (-1, -1), (-1, 1), (1, 1), (1, -1),
        (0, 2), (2, 0), (2, 1), (1, 2), (-1, 2), (2, -1), (2, 2),
    ]
    places = jnp.stack([(y_index + dy) % 4 * 4 + (z_index + dz) % 4 for dy, dz in names])
    places = places.astype(jnp.int32)
    states = [early, late]
    before = ring(jnp.concatenate([s[:, SHARE - PAD :] for s in states]), 1)
    after = ring(jnp.concatenate([s[:, :PAD] for s in states]), -1)
    window = assemble(states, before, after, places, mp_index)

    product = products(window, target, keep, step_gains)
    product = sum_dp(product, AROUND_Z)
    product = sum_dp(product, AROUND_Y)
    grad, error = gradients(window, target, keep, keep_row, step_gains, product, factor)

    arrived = [along_mp(grad, k, 0) for k in (1, 3, 2)]
    error = tie(error, arrived[0])
    error = sum_dp(sum_dp(error, AROUND_Z), AROUND_Y)
    error = error + sum(along_mp(error, k, 0) for k in (1, 3, 2))
    mine = tie(jnp.stack([grad] + arrived), error)
    other = along_mp(mine, 0, 1)
    owners = [(x_index - k) % 4 * 2 + c for c in (core, 1 - core) for k in (0, 1, 3, 2)]
    grad_weight = weight_gradient(
        [own_block, *round1, *round2, *round3, *round4], places, mine, other, owners
    )

    error = error + along_mp(error, 0, 1)
    mean_loss = error[0, 0] / (2.0 * D * (error[0, 1] / lax.axis_size("dp")))
    return (mean_loss, grad_weight)


def solution(mesh):
    in_specs = (P("dp", "mp"), P("mp", "dp"), P("mp", "dp"), P("mp"), P(None, "dp"))
    out_specs = (P(), P("mp", "dp"))
    return jax.shard_map(local, mesh=mesh, in_specs=in_specs, out_specs=out_specs, check_vma=False)
```

```python
import math

import jax
import jax.numpy as jnp
from jax import lax
from jax.experimental import pallas as pl
from jax.experimental.pallas import tpu as pltpu
from jax.sharding import PartitionSpec as P

D = 8192
STEPS = 3
EPSILON = 1e-06

SHARE = 32
PAD = 8
LENGTH = SHARE + 2 * PAD
BLOCKS = 16
PRODUCTS = 24
VMEM = 40 * 1024 * 1024


def from_dp(block, place):
    route = []
    for y in range(4):
        for z in range(4):
            sy, sz = place(y, z)
            route.append((sy % 4 * 4 + sz % 4, y * 4 + z))
    return lax.ppermute(block, "dp", route)


def along_mp(block, dx, dcore):
    route = [(x * 2 + c, (x + dx) % 4 * 2 + (c ^ dcore)) for x in range(4) for c in range(2)]
    return lax.ppermute(block, "mp", route)


def neighbour(block, distance):
    devices = range(lax.axis_size("mp"))
    route = [(i - distance, i) for i in devices if i - distance in devices]
    return lax.ppermute(block, "mp", route)


def down(block):
    return jnp.concatenate([block[-1:], block[:-1]], axis=0)


def up(block):
    return jnp.concatenate([block[1:], block[:1]], axis=0)


def before(row):
    return jnp.concatenate([row[:, -1:], row[:, :-1]], axis=1)


def after(row):
    return jnp.concatenate([row[:, 1:], row[:, :1]], axis=1)


def tie(value, *others):
    return lax.optimization_barrier((value, *others))[0]


FREE = pl.CostEstimate(flops=1, bytes_accessed=1, transcendentals=0)


def windows_kernel(block_rows, target_ref, out_ref):
    for owner in range(8):
        for block in range(2):
            start = block * block_rows + owner * SHARE + PAD
            out_ref[owner, block] = target_ref[start : start + LENGTH, :]


def windows(target, block_rows):
    return pl.pallas_call(
        lambda *refs: windows_kernel(block_rows, *refs),
        out_shape=jax.ShapeDtypeStruct((8, 2, LENGTH, target.shape[1]), target.dtype),
        in_specs=[pl.BlockSpec(memory_space=pltpu.VMEM)],
        out_specs=pl.BlockSpec(memory_space=pltpu.VMEM),
        compiler_params=pltpu.CompilerParams(vmem_limit_bytes=VMEM),
        cost_estimate=FREE,
        name="windows",
    )(target)


def product_kernel(state_ref, target_ref, keep_ref, gain_ref, out_ref, columns):
    gain0, gain1, gain2 = (gain_ref[k : k + 1, :] for k in range(STEPS))
    lane = lax.broadcasted_iota(jnp.int32, (LENGTH, 128), 1)

    def block(index, carry):
        state, target, keep = state_ref[index], target_ref[index], keep_ref[index]
        previous = down(state)
        mixed0 = state + keep * previous
        scaled0 = gain0 * down(mixed0)
        second = gain1 * previous
        third = gain1 * down(scaled0)
        target1 = up(target)
        target2 = gain2 * up(target1)
        weight = gain2 * gain2
        weighted, weighted2, weighted3 = weight * state, weight * second, weight * third
        pairs = [
            (mixed0, mixed0),
            (state, state),
            (state, scaled0),
            (scaled0, scaled0),
            (state, second),
            (state, third),
            (second, second),
            (second, third),
            (third, third),
            (weighted, state),
            (weighted, second),
            (weighted, third),
            (weighted2, second),
            (weighted2, third),
            (weighted3, third),
            (target2, state),
            (target2, second),
            (target2, third),
            (gain1 * target1, state),
            (gain1 * target1, scaled0),
            (gain0 * target, mixed0),
            (target, target),
        ]
        total = jnp.zeros((LENGTH, 128), jnp.float32)
        for k, (left, right) in enumerate(pairs):
            value = jnp.sum(left * right, axis=1, keepdims=True)
            total = jnp.where(lane == k, value, total)
        columns[pl.ds(pl.multiple_of(index * LENGTH, 8), LENGTH), :] = total
        return carry

    lax.fori_loop(0, BLOCKS, block, 0)
    out_ref[...] = columns[...].T[:PRODUCTS, :]


def products(state, target, keep, gains):
    lanes = BLOCKS * LENGTH
    return pl.pallas_call(
        product_kernel,
        out_shape=jax.ShapeDtypeStruct((PRODUCTS, lanes), jnp.float32),
        in_specs=[pl.BlockSpec(memory_space=pltpu.VMEM)] * 4,
        out_specs=pl.BlockSpec(memory_space=pltpu.VMEM),
        scratch_shapes=[pltpu.VMEM((lanes, 128), jnp.float32)],
        compiler_params=pltpu.CompilerParams(vmem_limit_bytes=VMEM),
        cost_estimate=FREE,
        name="products",
    )(state, target, keep, gains)


def coefficients(product, keep, factor):
    p = [None] + [product[k : k + 1, :] for k in range(22)]

    def scale(squares):
        return lax.rsqrt(jnp.maximum(squares, 0.0) / D + EPSILON)

    scale0 = scale(p[1])
    r0 = keep * before(scale0)
    scale1 = scale(p[2] + 2.0 * r0 * p[3] + r0 * r0 * p[4])
    a = keep * before(scale1)
    b = a * before(r0)
    scale2 = scale(
        p[2] + a * a * p[7] + b * b * p[9] + 2.0 * a * p[5] + 2.0 * b * p[6] + 2.0 * a * b * p[8]
    )
    same_next = after(keep)
    same_second = same_next * after(same_next)
    x1 = p[10] + a * p[11] + b * p[12]
    x2 = p[11] + a * p[13] + b * p[14]
    x3 = p[12] + a * p[14] + b * p[15]
    product2 = (
        factor
        * same_second
        * scale2
        * (scale2 * (x1 + a * x2 + b * x3) - (p[16] + a * p[17] + b * p[18]))
    )
    alpha2 = factor * same_second * scale2 * scale2
    gamma2 = -factor * same_second * scale2
    beta2 = -scale2 * scale2 * product2 / D
    second = alpha2 * x2 + beta2 * (p[5] + a * p[7] + b * p[8]) + gamma2 * p[17]
    third = alpha2 * x3 + beta2 * (p[6] + a * p[8] + b * p[9]) + gamma2 * p[18]
    next7, next8, next9 = after(p[7]), after(p[8]), after(p[9])
    y1 = next7 + r0 * next8
    y2 = next8 + r0 * next9
    product1 = scale1 * (
        factor * same_next * (scale1 * (y1 + r0 * y2) - (p[19] + r0 * p[20]))
        + same_next * (after(second) + r0 * after(third))
    )
    alpha1 = factor * same_next * scale1 * scale1
    gamma1 = -factor * same_next * scale1
    eta1 = scale1 * same_next
    beta1 = -scale1 * scale1 * product1 / D
    carried = alpha1 * y2 + gamma1 * p[20] + eta1 * after(third) + beta1 * (p[3] + r0 * p[4])
    product0 = scale0 * (
        factor * (scale0 * after(p[4]) - p[21]) + same_next * after(carried)
    )
    alpha0 = factor * scale0 * scale0
    gamma0 = -factor * scale0
    eta0 = scale0 * same_next
    beta0 = -scale0 * scale0 * product0 / D
    goal0 = p[22]
    goal1, goal2 = after(goal0), after(after(goal0))
    squares = (
        scale0 * (scale0 * after(p[4]) - 2.0 * p[21])
        + goal0
        + same_next * (scale1 * (scale1 * (y1 + r0 * y2) - 2.0 * (p[19] + r0 * p[20])) + goal1)
        + same_second
        * (
            scale2 * (scale2 * (x1 + a * x2 + b * x3) - 2.0 * (p[16] + a * p[17] + b * p[18]))
            + goal2
        )
    )
    count = 1.0 + same_next + same_second
    table = [
        r0, a, b, same_next,
        alpha2, beta2, gamma2, alpha1, beta1, gamma1, eta1, alpha0, beta0, gamma0, eta0,
    ]
    return table, squares, count


def gradient_kernel(factor, state_ref, target_ref, keep_ref, keep_row_ref, gain_ref, *refs):
    product_refs, (grad_ref, table, columns) = refs[:4], refs[4:]
    product = product_refs[0][...]
    for ref in product_refs[1:]:
        product = product + ref[...]
    gain0, gain1, gain2 = (gain_ref[k : k + 1, :] for k in range(STEPS))
    table[...] = jnp.zeros_like(table)
    found, squares, count = coefficients(product, keep_row_ref[...], factor)
    for k, row in enumerate(found):
        table[k : k + 1, :] = row
    columns[...] = table[...].T

    def block(index, carry):
        state, target, keep = state_ref[index], target_ref[index], keep_ref[index]
        values = columns[pl.ds(pl.multiple_of(index * LENGTH, 8), LENGTH), :]
        (
            r0, a, b, same_next,
            alpha2, beta2, gamma2, alpha1, beta1, gamma1, eta1, alpha0, beta0, gamma0, eta0,
        ) = (values[:, k : k + 1] for k in range(len(found)))
        previous = down(state)
        mixed0 = state + keep * previous
        scaled0 = gain0 * down(mixed0)
        mixed1 = state + r0 * scaled0
        mixed2 = state + gain1 * (a * previous + b * down(scaled0))
        target1 = up(target)
        target2 = up(target1)
        grad2 = (alpha2 * (gain2 * gain2) + beta2) * mixed2 + gamma2 * (gain2 * target2)
        grad1 = (alpha1 * (gain1 * gain1) + beta1) * mixed1 + gain1 * (
            gamma1 * target1 + eta1 * up(grad2)
        )
        grad0 = (alpha0 * (gain0 * gain0) + beta0) * mixed0 + gain0 * (
            gamma0 * target + eta0 * up(grad1)
        )
        grad = grad0 + grad1 + grad2 + same_next * up(grad0)
        grad_ref[index] = grad[PAD : PAD + SHARE].astype(jnp.bfloat16)
        return carry

    lax.fori_loop(0, BLOCKS, block, 0)
    place = lax.broadcasted_iota(jnp.int32, squares.shape, 1) % LENGTH
    own_rows = (place >= PAD) & (place < PAD + SHARE)
    parts = []
    for value in (squares, count):
        value = jnp.sum(jnp.where(own_rows, value, 0.0), axis=1, keepdims=True)
        for _ in range(3):
            part = value.astype(jnp.bfloat16).astype(jnp.float32)
            parts.append(part)
            value = value - part
    lane = lax.broadcasted_iota(jnp.int32, grad_ref.shape[1:], 1)
    sums = jnp.zeros(lane.shape, jnp.float32)
    for i, part in enumerate(parts):
        sums = jnp.where(lane == i, part, sums)
    grad_ref[BLOCKS] = sums.astype(jnp.bfloat16)


def gradients(state, target, keep, keep_row, gains, product, factor):
    lanes = product[0].shape[1]
    return pl.pallas_call(
        lambda *refs: gradient_kernel(factor, *refs),
        out_shape=jax.ShapeDtypeStruct((BLOCKS + 1, SHARE, state.shape[2]), jnp.bfloat16),
        in_specs=[pl.BlockSpec(memory_space=pltpu.VMEM)] * 9,
        out_specs=pl.BlockSpec(memory_space=pltpu.VMEM),
        scratch_shapes=[
            pltpu.VMEM((128, lanes), jnp.float32),
            pltpu.VMEM((lanes, 128), jnp.float32),
        ],
        compiler_params=pltpu.CompilerParams(vmem_limit_bytes=VMEM),
        cost_estimate=FREE,
        name="gradients",
    )(state, target, keep, keep_row, gains, *product)


def project_kernel(pieces, blocks, core_ref, weight_ref, *refs):
    rows, (send_ref, keep_ref, total) = refs[:pieces], refs[pieces:]
    total[...] = jnp.dot(
        jnp.concatenate([r[...] for r in rows], axis=0),
        weight_ref[...],
        preferred_element_type=jnp.float32,
    )
    core = core_ref[0]
    for x in range(4):
        for block in range(blocks):
            start = (block * 4 + x) * 2 * SHARE
            keep = pl.ds(pl.multiple_of(start + core * SHARE, SHARE), SHARE)
            send = pl.ds(pl.multiple_of(start + (1 - core) * SHARE, SHARE), SHARE)
            keep_ref[x, block] = total[keep, :]
            send_ref[x, block] = total[send, :].astype(jnp.bfloat16)


def project(rows, weight, core):
    columns = weight.shape[1]
    tokens = sum(r.shape[0] for r in rows)
    blocks = tokens // (8 * SHARE)
    shape = (4, blocks, SHARE, columns)
    return pl.pallas_call(
        lambda *refs: project_kernel(len(rows), blocks, *refs),
        out_shape=(
            jax.ShapeDtypeStruct(shape, jnp.bfloat16),
            jax.ShapeDtypeStruct(shape, jnp.float32),
        ),
        in_specs=[pl.BlockSpec(memory_space=pltpu.SMEM)]
        + [pl.BlockSpec(memory_space=pltpu.VMEM)] * (len(rows) + 1),
        out_specs=(pl.BlockSpec(memory_space=pltpu.VMEM),) * 2,
        scratch_shapes=[pltpu.VMEM((tokens, columns), jnp.float32)],
        compiler_params=pltpu.CompilerParams(vmem_limit_bytes=VMEM),
        cost_estimate=FREE,
        name="project",
    )(jnp.stack([core]).astype(jnp.int32), weight, *rows)


def assemble_kernel(groups, place_ref, owner_ref, *refs):
    states, (before_ref, after_ref, window_ref) = refs[:groups], refs[groups:]
    first = (owner_ref[0] == 0).astype(jnp.int32)
    last = (owner_ref[0] == 7).astype(jnp.int32)
    edge = jnp.zeros((PAD, window_ref.shape[2]), jnp.float32)
    window_ref[0, :PAD] = edge
    window_ref[BLOCKS - 1, PAD + SHARE :] = edge
    k = 0
    for state_ref in states:
        for i in range(state_ref.shape[0]):
            block = place_ref[k]
            window_ref[block, PAD : PAD + SHARE] = state_ref[i]

            @pl.when(block + first < BLOCKS)
            def _():
                window_ref[jnp.minimum(block + first, BLOCKS - 1), :PAD] = before_ref[k]

            @pl.when(block >= last)
            def _():
                window_ref[jnp.maximum(block - last, 0), PAD + SHARE :] = after_ref[k]

            k += 1


def assemble(states, before, after, places, owner):
    return pl.pallas_call(
        lambda *refs: assemble_kernel(len(states), *refs),
        out_shape=jax.ShapeDtypeStruct((BLOCKS, LENGTH, before.shape[2]), jnp.float32),
        in_specs=[pl.BlockSpec(memory_space=pltpu.SMEM)] * 2
        + [pl.BlockSpec(memory_space=pltpu.VMEM)] * (len(states) + 2),
        out_specs=pl.BlockSpec(memory_space=pltpu.VMEM),
        compiler_params=pltpu.CompilerParams(vmem_limit_bytes=VMEM),
        cost_estimate=FREE,
        name="assemble",
    )(places, jnp.stack([owner]).astype(jnp.int32), *states, before, after)


def weight_kernel(pieces, block_ref, owner_ref, *refs):
    rows, grads = refs[:pieces], refs[pieces : pieces + 8]
    out_ref, loss_ref, ordered = refs[pieces + 8 :]

    @pl.when(pl.program_id(0) == 0)
    def _():
        for i, grad_ref in enumerate(grads):
            for k in range(BLOCKS):
                start = pl.multiple_of((k * 8 + owner_ref[i]) * SHARE, SHARE)
                ordered[pl.ds(start, SHARE), :] = grad_ref[block_ref[k]]
        sums = sum(grad_ref[BLOCKS].astype(jnp.float32) for grad_ref in grads)
        row = lax.broadcasted_iota(jnp.int32, sums.shape, 0)
        lane = lax.broadcasted_iota(jnp.int32, sums.shape, 1)
        error = jnp.sum(jnp.where((row == 0) & (lane < 3), sums, 0.0))
        count = jnp.sum(jnp.where((row == 0) & (lane >= 3) & (lane < 6), sums, 0.0))
        loss_ref[...] = jnp.full(loss_ref.shape, error / (2.0 * D * count), jnp.float32)

    out_ref[...] = lax.dot_general(
        jnp.concatenate([r[...] for r in rows], axis=0),
        ordered[...],
        (((0,), (0,)), ((), ())),
        preferred_element_type=jnp.float32,
    )


def weight_gradient(rows, blocks, grads, owners):
    features, columns = rows[0].shape[1], grads[0].shape[2]
    tokens = sum(r.shape[0] for r in rows)
    width = 512
    return pl.pallas_call(
        lambda *refs: weight_kernel(len(rows), *refs),
        out_shape=(
            jax.ShapeDtypeStruct((features, columns), jnp.float32),
            jax.ShapeDtypeStruct((1, 128), jnp.float32),
        ),
        grid_spec=pltpu.PrefetchScalarGridSpec(
            num_scalar_prefetch=2,
            grid=(features // width,),
            in_specs=[pl.BlockSpec((r.shape[0], width), lambda i, *_: (0, i)) for r in rows]
            + [pl.BlockSpec(g.shape, lambda i, *_: (0, 0, 0)) for g in grads],
            out_specs=(
                pl.BlockSpec((width, columns), lambda i, *_: (i, 0)),
                pl.BlockSpec((1, 128), lambda i, *_: (0, 0)),
            ),
            scratch_shapes=[pltpu.VMEM((tokens, columns), jnp.bfloat16)],
        ),
        compiler_params=pltpu.CompilerParams(vmem_limit_bytes=VMEM),
        cost_estimate=FREE,
        name="weight_gradient",
    )(blocks, jnp.stack(owners).astype(jnp.int32), *rows, *grads)


def sum_dp(value, places):
    return value + sum(from_dp(value, place) for place in places)


AROUND_Z = tuple(lambda y, z, k=k: (y, z + k) for k in (1, 3, 2))
AROUND_Y = tuple(lambda y, z, k=k: (y + k, z) for k in (1, 3, 2))


def step(block, dy, dz):
    return from_dp(block, lambda y, z: (y + dy, z + dz))


def ring(block, distance):
    return lax.ppermute(block, "mp", [((i - distance) % 8, i) for i in range(8)])


def local(joined_rows, fc_weight, target_features, segment_ids, step_gains):
    mp_index = lax.axis_index("mp")
    x_index, core = mp_index // 2, mp_index % 2
    dp_index = lax.axis_index("dp")
    y_index, z_index = dp_index // 4, dp_index % 4
    own, columns = target_features.shape
    block_rows = joined_rows.shape[0]
    total_rows = block_rows * lax.axis_size("dp")
    factor = 1.0 / math.sqrt(total_rows)
    barrier = lax.optimization_barrier

    def chip_sum(rows):
        send, kept = project(rows, fc_weight, core)
        return kept + along_mp(send, 0, 1).astype(jnp.float32)

    def first_state(summed):
        parts = [
            lax.dynamic_index_in_dim(summed, (x_index + k) % 4, 0, keepdims=False)
            for k in (0, 1, 3, 2)
        ]
        return parts[0] + sum(
            along_mp(part.astype(jnp.bfloat16), k, 0).astype(jnp.float32)
            for part, k in zip(parts[1:], (1, 3, 2))
        )

    own_block = joined_rows
    round1 = (
        step(own_block, 0, -1), step(own_block, 0, 1),
        step(own_block, -1, 0), step(own_block, 1, 0),
    )
    next_target = neighbour(target_features[: 2 * PAD], -1)
    next_segments = neighbour(segment_ids[: 2 * PAD], -1)
    last_segments = neighbour(segment_ids[-2 * PAD - 1 :], 1)
    round1, next_target, next_segments, last_segments = barrier(
        (round1, next_target, next_segments, last_segments)
    )
    b0m, b01, bm0, b10 = round1
    round2 = (step(b0m, -1, 0), step(bm0, 0, 1), step(b01, 1, 0), step(b10, 0, -1))

    segments = jnp.concatenate([last_segments, segment_ids, next_segments])
    token = mp_index * own - 2 * PAD + jnp.arange(own + 4 * PAD, dtype=jnp.int32)
    keep = (segments[1:] == segments[:-1]) & (token > 0) & (token < total_rows)
    target = jnp.concatenate(
        [jnp.zeros((2 * PAD, columns), jnp.bfloat16), target_features, next_target]
    )
    target = jnp.concatenate(
        [target, jnp.broadcast_to(keep.astype(jnp.bfloat16)[:, None], (target.shape[0], 128))],
        axis=1,
    )
    shares = lax.all_to_all(windows(target, block_rows), "mp", 0, 0, tiled=True)
    round2, shares = barrier((round2, shares))
    shares = shares.reshape(BLOCKS, LENGTH, columns + 128)
    target = shares[..., :columns].astype(jnp.float32)
    keep = shares[..., columns : columns + 1].astype(jnp.float32)
    keep_row = keep.reshape(1, BLOCKS * LENGTH)

    bmm, bm1, b11, b1m = round2
    round3 = (step(b0m, 0, -1), step(bm0, -1, 0), step(b11, 1, 0), step(b11, 0, 1))
    early = chip_sum([own_block, *round1, *round2])
    round3, early = barrier((round3, early))
    early = first_state(early)
    b02, b20, b21, b12 = round3
    round4 = (step(bmm, 0, -1), step(bmm, -1, 0), step(b21, 0, 1))
    middle = chip_sum(round3)
    round4, early, middle, target, keep, keep_row = barrier(
        (round4, early, middle, target, keep, keep_row)
    )
    late = first_state(jnp.concatenate([middle, chip_sum(round4)], axis=1))

    names = [
        (0, 0), (0, -1), (0, 1), (-1, 0), (1, 0), (-1, -1), (-1, 1), (1, 1), (1, -1),
        (0, 2), (2, 0), (2, 1), (1, 2), (-1, 2), (2, -1), (2, 2),
    ]
    places = jnp.stack([(y_index + dy) % 4 * 4 + (z_index + dz) % 4 for dy, dz in names])
    places = places.astype(jnp.int32)
    states = [early, late]
    before = ring(jnp.concatenate([s[:, SHARE - PAD :] for s in states]), 1)
    after = ring(jnp.concatenate([s[:, :PAD] for s in states]), -1)
    window = assemble(states, before, after, places, mp_index)

    product = products(window, target, keep, step_gains)
    product = sum_dp(product, AROUND_Z)
    product = [product] + [from_dp(product, place) for place in AROUND_Y]
    grad = gradients(window, target, keep, keep_row, step_gains, product, factor)

    grads = [grad] + [along_mp(grad, k, 0) for k in (1, 3, 2)]
    grads = grads + [along_mp(g, 0, 1) for g in grads]
    owners = [(x_index - k) % 4 * 2 + c for c in (core, 1 - core) for k in (0, 1, 3, 2)]
    grad_weight, mean_loss = weight_gradient(
        [own_block, *round1, *round2, *round3, *round4], places, grads, owners
    )
    mean_loss = mean_loss[0, 0]
    return (mean_loss, grad_weight)


def solution(mesh):
    in_specs = (P("dp", "mp"), P("mp", "dp"), P("mp", "dp"), P("mp"), P(None, "dp"))
    out_specs = (P(), P("mp", "dp"))
    return jax.shard_map(local, mesh=mesh, in_specs=in_specs, out_specs=out_specs, check_vma=False)
```

```python
import math

import jax
import jax.numpy as jnp
from jax import lax
from jax.experimental import pallas as pl
from jax.experimental.pallas import tpu as pltpu
from jax.sharding import PartitionSpec as P

D = 8192
STEPS = 3
EPSILON = 1e-06

SHARE = 32
PAD = 8
LENGTH = SHARE + 2 * PAD
BLOCKS = 16
PRODUCTS = 24
MIB = 1024 * 1024


def from_dp(block, place):
    route = []
    for y in range(4):
        for z in range(4):
            sy, sz = place(y, z)
            route.append((sy % 4 * 4 + sz % 4, y * 4 + z))
    return lax.ppermute(block, "dp", route)


def along_mp(block, dx, dcore):
    route = [(x * 2 + c, (x + dx) % 4 * 2 + (c ^ dcore)) for x in range(4) for c in range(2)]
    return lax.ppermute(block, "mp", route)


def neighbour(block, distance):
    devices = range(lax.axis_size("mp"))
    route = [(i - distance, i) for i in devices if i - distance in devices]
    return lax.ppermute(block, "mp", route)


def down(block):
    return jnp.concatenate([block[-1:], block[:-1]], axis=0)


def up(block):
    return jnp.concatenate([block[1:], block[:1]], axis=0)


def before(row):
    return jnp.concatenate([row[:, -1:], row[:, :-1]], axis=1)


def after(row):
    return jnp.concatenate([row[:, 1:], row[:, :1]], axis=1)


def tie(value, *others):
    return lax.optimization_barrier((value, *others))[0]


FREE = pl.CostEstimate(flops=1, bytes_accessed=1, transcendentals=0)


def windows_kernel(block_rows, target_ref, out_ref):
    for owner in range(8):
        for block in range(2):
            start = block * block_rows + owner * SHARE + PAD
            out_ref[owner, block] = target_ref[start : start + LENGTH, :]


def windows(target, block_rows):
    return pl.pallas_call(
        lambda *refs: windows_kernel(block_rows, *refs),
        out_shape=jax.ShapeDtypeStruct((8, 2, LENGTH, target.shape[1]), target.dtype),
        in_specs=[pl.BlockSpec(memory_space=pltpu.VMEM)],
        out_specs=pl.BlockSpec(memory_space=pltpu.VMEM),
        compiler_params=pltpu.CompilerParams(vmem_limit_bytes=8 * MIB),
        cost_estimate=FREE,
        name="windows",
    )(target)


def product_kernel(state_ref, target_ref, keep_ref, gain_ref, out_ref, columns):
    gain0, gain1, gain2 = (gain_ref[k : k + 1, :] for k in range(STEPS))
    lane = lax.broadcasted_iota(jnp.int32, (LENGTH, 128), 1)

    def block(index, carry):
        state, target, keep = state_ref[index], target_ref[index], keep_ref[index]
        previous = down(state)
        mixed0 = state + keep * previous
        scaled0 = gain0 * down(mixed0)
        second = gain1 * previous
        third = gain1 * down(scaled0)
        target1 = up(target)
        target2 = gain2 * up(target1)
        weight = gain2 * gain2
        weighted, weighted2, weighted3 = weight * state, weight * second, weight * third
        pairs = [
            (mixed0, mixed0),
            (state, state),
            (state, scaled0),
            (scaled0, scaled0),
            (state, second),
            (state, third),
            (second, second),
            (second, third),
            (third, third),
            (weighted, state),
            (weighted, second),
            (weighted, third),
            (weighted2, second),
            (weighted2, third),
            (weighted3, third),
            (target2, state),
            (target2, second),
            (target2, third),
            (gain1 * target1, state),
            (gain1 * target1, scaled0),
            (gain0 * target, mixed0),
            (target, target),
        ]
        total = jnp.zeros((LENGTH, 128), jnp.float32)
        for k, (left, right) in enumerate(pairs):
            value = jnp.sum(left * right, axis=1, keepdims=True)
            total = jnp.where(lane == k, value, total)
        columns[pl.ds(pl.multiple_of(index * LENGTH, 8), LENGTH), :] = total
        return carry

    lax.fori_loop(0, BLOCKS, block, 0)
    out_ref[...] = columns[...].T[:PRODUCTS, :]


def products(state, target, keep, gains):
    lanes = BLOCKS * LENGTH
    return pl.pallas_call(
        product_kernel,
        out_shape=jax.ShapeDtypeStruct((PRODUCTS, lanes), jnp.float32),
        in_specs=[pl.BlockSpec(memory_space=pltpu.VMEM)] * 4,
        out_specs=pl.BlockSpec(memory_space=pltpu.VMEM),
        scratch_shapes=[pltpu.VMEM((lanes, 128), jnp.float32)],
        compiler_params=pltpu.CompilerParams(vmem_limit_bytes=12 * MIB),
        cost_estimate=FREE,
        name="products",
    )(state, target, keep, gains)


def coefficients(product, keep, factor):
    p = [None] + [product[k : k + 1, :] for k in range(22)]

    def scale(squares):
        return lax.rsqrt(jnp.maximum(squares, 0.0) / D + EPSILON)

    scale0 = scale(p[1])
    r0 = keep * before(scale0)
    scale1 = scale(p[2] + 2.0 * r0 * p[3] + r0 * r0 * p[4])
    a = keep * before(scale1)
    b = a * before(r0)
    scale2 = scale(
        p[2] + a * a * p[7] + b * b * p[9] + 2.0 * a * p[5] + 2.0 * b * p[6] + 2.0 * a * b * p[8]
    )
    same_next = after(keep)
    same_second = same_next * after(same_next)
    x1 = p[10] + a * p[11] + b * p[12]
    x2 = p[11] + a * p[13] + b * p[14]
    x3 = p[12] + a * p[14] + b * p[15]
    product2 = (
        factor
        * same_second
        * scale2
        * (scale2 * (x1 + a * x2 + b * x3) - (p[16] + a * p[17] + b * p[18]))
    )
    alpha2 = factor * same_second * scale2 * scale2
    gamma2 = -factor * same_second * scale2
    beta2 = -scale2 * scale2 * product2 / D
    second = alpha2 * x2 + beta2 * (p[5] + a * p[7] + b * p[8]) + gamma2 * p[17]
    third = alpha2 * x3 + beta2 * (p[6] + a * p[8] + b * p[9]) + gamma2 * p[18]
    next7, next8, next9 = after(p[7]), after(p[8]), after(p[9])
    y1 = next7 + r0 * next8
    y2 = next8 + r0 * next9
    product1 = scale1 * (
        factor * same_next * (scale1 * (y1 + r0 * y2) - (p[19] + r0 * p[20]))
        + same_next * (after(second) + r0 * after(third))
    )
    alpha1 = factor * same_next * scale1 * scale1
    gamma1 = -factor * same_next * scale1
    eta1 = scale1 * same_next
    beta1 = -scale1 * scale1 * product1 / D
    carried = alpha1 * y2 + gamma1 * p[20] + eta1 * after(third) + beta1 * (p[3] + r0 * p[4])
    product0 = scale0 * (
        factor * (scale0 * after(p[4]) - p[21]) + same_next * after(carried)
    )
    alpha0 = factor * scale0 * scale0
    gamma0 = -factor * scale0
    eta0 = scale0 * same_next
    beta0 = -scale0 * scale0 * product0 / D
    goal0 = p[22]
    goal1, goal2 = after(goal0), after(after(goal0))
    squares = (
        scale0 * (scale0 * after(p[4]) - 2.0 * p[21])
        + goal0
        + same_next * (scale1 * (scale1 * (y1 + r0 * y2) - 2.0 * (p[19] + r0 * p[20])) + goal1)
        + same_second
        * (
            scale2 * (scale2 * (x1 + a * x2 + b * x3) - 2.0 * (p[16] + a * p[17] + b * p[18]))
            + goal2
        )
    )
    count = 1.0 + same_next + same_second
    table = [
        r0, a, b, same_next,
        alpha2, beta2, gamma2, alpha1, beta1, gamma1, eta1, alpha0, beta0, gamma0, eta0,
    ]
    return table, squares, count


def gradient_kernel(factor, state_ref, target_ref, keep_ref, keep_row_ref, gain_ref, *refs):
    product_refs, (low_ref, high_ref, table, columns) = refs[:4], refs[4:]
    product = product_refs[0][...]
    for ref in product_refs[1:]:
        product = product + ref[...]
    gain0, gain1, gain2 = (gain_ref[k : k + 1, :] for k in range(STEPS))
    table[...] = jnp.zeros_like(table)
    found, squares, count = coefficients(product, keep_row_ref[...], factor)
    for k, row in enumerate(found):
        table[k : k + 1, :] = row
    columns[...] = table[...].T

    def block(index, grad_ref, first):
        state, target, keep = state_ref[index], target_ref[index], keep_ref[index]
        values = columns[pl.ds(pl.multiple_of(index * LENGTH, 8), LENGTH), :]
        (
            r0, a, b, same_next,
            alpha2, beta2, gamma2, alpha1, beta1, gamma1, eta1, alpha0, beta0, gamma0, eta0,
        ) = (values[:, k : k + 1] for k in range(len(found)))
        previous = down(state)
        mixed0 = state + keep * previous
        scaled0 = gain0 * down(mixed0)
        mixed1 = state + r0 * scaled0
        mixed2 = state + gain1 * (a * previous + b * down(scaled0))
        target1 = up(target)
        target2 = up(target1)
        grad2 = (alpha2 * (gain2 * gain2) + beta2) * mixed2 + gamma2 * (gain2 * target2)
        grad1 = (alpha1 * (gain1 * gain1) + beta1) * mixed1 + gain1 * (
            gamma1 * target1 + eta1 * up(grad2)
        )
        grad0 = (alpha0 * (gain0 * gain0) + beta0) * mixed0 + gain0 * (
            gamma0 * target + eta0 * up(grad1)
        )
        grad = grad0 + grad1 + grad2 + same_next * up(grad0)
        grad_ref[index - first] = grad[PAD : PAD + SHARE].astype(jnp.bfloat16)

    half = BLOCKS // 2
    pl.loop(0, half)(lambda index: block(index, low_ref, 0))
    pl.loop(half, BLOCKS)(lambda index: block(index, high_ref, half))
    place = lax.broadcasted_iota(jnp.int32, squares.shape, 1) % LENGTH
    own_rows = (place >= PAD) & (place < PAD + SHARE)
    parts = []
    for value in (squares, count):
        value = jnp.sum(jnp.where(own_rows, value, 0.0), axis=1, keepdims=True)
        for _ in range(3):
            part = value.astype(jnp.bfloat16).astype(jnp.float32)
            parts.append(part)
            value = value - part
    lane = lax.broadcasted_iota(jnp.int32, high_ref.shape[1:], 1)
    sums = jnp.zeros(lane.shape, jnp.float32)
    for i, part in enumerate(parts):
        sums = jnp.where(lane == i, part, sums)
    high_ref[half] = sums.astype(jnp.bfloat16)


def gradients(state, target, keep, keep_row, gains, product, factor):
    lanes = product[0].shape[1]
    return pl.pallas_call(
        lambda *refs: gradient_kernel(factor, *refs),
        out_shape=tuple(
            jax.ShapeDtypeStruct((BLOCKS // 2 + more, SHARE, state.shape[2]), jnp.bfloat16)
            for more in (0, 1)
        ),
        in_specs=[pl.BlockSpec(memory_space=pltpu.VMEM)] * 9,
        out_specs=(pl.BlockSpec(memory_space=pltpu.VMEM),) * 2,
        scratch_shapes=[
            pltpu.VMEM((128, lanes), jnp.float32),
            pltpu.VMEM((lanes, 128), jnp.float32),
        ],
        compiler_params=pltpu.CompilerParams(vmem_limit_bytes=12 * MIB),
        cost_estimate=FREE,
        name="gradients",
    )(state, target, keep, keep_row, gains, *product)


def project_kernel(pieces, blocks, core_ref, weight_ref, *refs):
    rows, (send_ref, keep_ref, total) = refs[:pieces], refs[pieces:]
    total[...] = jnp.dot(
        jnp.concatenate([r[...] for r in rows], axis=0),
        weight_ref[...],
        preferred_element_type=jnp.float32,
    )
    core = core_ref[0]
    for x in range(4):
        for block in range(blocks):
            start = (block * 4 + x) * 2 * SHARE
            keep = pl.ds(pl.multiple_of(start + core * SHARE, SHARE), SHARE)
            send = pl.ds(pl.multiple_of(start + (1 - core) * SHARE, SHARE), SHARE)
            keep_ref[x, block] = total[keep, :]
            send_ref[x, block] = total[send, :].astype(jnp.bfloat16)


def project(rows, weight, core):
    columns = weight.shape[1]
    tokens = sum(r.shape[0] for r in rows)
    blocks = tokens // (8 * SHARE)
    shape = (4, blocks, SHARE, columns)
    return pl.pallas_call(
        lambda *refs: project_kernel(len(rows), blocks, *refs),
        out_shape=(
            jax.ShapeDtypeStruct(shape, jnp.bfloat16),
            jax.ShapeDtypeStruct(shape, jnp.float32),
        ),
        in_specs=[pl.BlockSpec(memory_space=pltpu.SMEM)]
        + [pl.BlockSpec(memory_space=pltpu.VMEM)] * (len(rows) + 1),
        out_specs=(pl.BlockSpec(memory_space=pltpu.VMEM),) * 2,
        scratch_shapes=[pltpu.VMEM((tokens, columns), jnp.float32)],
        compiler_params=pltpu.CompilerParams(vmem_limit_bytes=32 * MIB),
        cost_estimate=FREE,
        name="project",
    )(jnp.stack([core]).astype(jnp.int32), weight, *rows)


def assemble_kernel(groups, place_ref, owner_ref, *refs):
    states, (before_ref, after_ref, window_ref) = refs[:groups], refs[groups:]
    first = (owner_ref[0] == 0).astype(jnp.int32)
    last = (owner_ref[0] == 7).astype(jnp.int32)
    edge = jnp.zeros((PAD, window_ref.shape[2]), jnp.float32)
    window_ref[0, :PAD] = edge
    window_ref[BLOCKS - 1, PAD + SHARE :] = edge
    k = 0
    for state_ref in states:
        for i in range(state_ref.shape[0]):
            block = place_ref[k]
            window_ref[block, PAD : PAD + SHARE] = state_ref[i]

            @pl.when(block + first < BLOCKS)
            def _():
                window_ref[jnp.minimum(block + first, BLOCKS - 1), :PAD] = before_ref[k]

            @pl.when(block >= last)
            def _():
                window_ref[jnp.maximum(block - last, 0), PAD + SHARE :] = after_ref[k]

            k += 1


def assemble(states, before, after, places, owner):
    return pl.pallas_call(
        lambda *refs: assemble_kernel(len(states), *refs),
        out_shape=jax.ShapeDtypeStruct((BLOCKS, LENGTH, before.shape[2]), jnp.float32),
        in_specs=[pl.BlockSpec(memory_space=pltpu.SMEM)] * 2
        + [pl.BlockSpec(memory_space=pltpu.VMEM)] * (len(states) + 2),
        out_specs=pl.BlockSpec(memory_space=pltpu.VMEM),
        compiler_params=pltpu.CompilerParams(vmem_limit_bytes=12 * MIB),
        cost_estimate=FREE,
        name="assemble",
    )(places, jnp.stack([owner]).astype(jnp.int32), *states, before, after)


def weight_kernel(pieces, position_ref, owner_ref, *refs):
    rows, grads = refs[:pieces], refs[pieces : pieces + 16]
    out_ref, loss_ref, ordered = refs[pieces + 16 :]
    half = BLOCKS // 2

    @pl.when(pl.program_id(0) == 0)
    def _():
        for i in range(8):
            for block in range(BLOCKS):
                start = (position_ref[block] * 8 + owner_ref[i]) * SHARE
                grad = grads[2 * i + block // half][block % half]
                ordered[pl.ds(pl.multiple_of(start, SHARE), SHARE), :] = grad
        sums = sum(grad_ref[half].astype(jnp.float32) for grad_ref in grads[1::2])
        row = lax.broadcasted_iota(jnp.int32, sums.shape, 0)
        lane = lax.broadcasted_iota(jnp.int32, sums.shape, 1)
        error = jnp.sum(jnp.where((row == 0) & (lane < 3), sums, 0.0))
        count = jnp.sum(jnp.where((row == 0) & (lane >= 3) & (lane < 6), sums, 0.0))
        loss_ref[...] = jnp.full(loss_ref.shape, error / (2.0 * D * count), jnp.float32)

    out_ref[...] = lax.dot_general(
        jnp.concatenate([r[...] for r in rows], axis=0),
        ordered[...],
        (((0,), (0,)), ((), ())),
        preferred_element_type=jnp.float32,
    )


def weight_gradient(rows, positions, grads, owners):
    features, columns = rows[0].shape[1], grads[0].shape[2]
    tokens = sum(r.shape[0] for r in rows)
    width = 512
    return pl.pallas_call(
        lambda *refs: weight_kernel(len(rows), *refs),
        out_shape=(
            jax.ShapeDtypeStruct((features, columns), jnp.float32),
            jax.ShapeDtypeStruct((1, 128), jnp.float32),
        ),
        grid_spec=pltpu.PrefetchScalarGridSpec(
            num_scalar_prefetch=2,
            grid=(features // width,),
            in_specs=[pl.BlockSpec((r.shape[0], width), lambda i, *_: (0, i)) for r in rows]
            + [pl.BlockSpec(g.shape, lambda i, *_: (0, 0, 0)) for g in grads],
            out_specs=(
                pl.BlockSpec((width, columns), lambda i, *_: (i, 0)),
                pl.BlockSpec((1, 128), lambda i, *_: (0, 0)),
            ),
            scratch_shapes=[pltpu.VMEM((tokens, columns), jnp.bfloat16)],
        ),
        compiler_params=pltpu.CompilerParams(vmem_limit_bytes=58 * MIB),
        cost_estimate=FREE,
        name="weight_gradient",
    )(positions, jnp.stack(owners).astype(jnp.int32), *rows, *grads)


def sum_dp(value, places):
    return value + sum(from_dp(value, place) for place in places)


AROUND_Z = tuple(lambda y, z, k=k: (y, z + k) for k in (1, 3, 2))
AROUND_Y = tuple(lambda y, z, k=k: (y + k, z) for k in (1, 3, 2))


def step(block, dy, dz):
    return from_dp(block, lambda y, z: (y + dy, z + dz))


def ring(block, distance):
    return lax.ppermute(block, "mp", [((i - distance) % 8, i) for i in range(8)])


def local(joined_rows, fc_weight, target_features, segment_ids, step_gains):
    mp_index = lax.axis_index("mp")
    x_index, core = mp_index // 2, mp_index % 2
    dp_index = lax.axis_index("dp")
    y_index, z_index = dp_index // 4, dp_index % 4
    own, columns = target_features.shape
    block_rows = joined_rows.shape[0]
    total_rows = block_rows * lax.axis_size("dp")
    factor = 1.0 / math.sqrt(total_rows)
    barrier = lax.optimization_barrier

    def chip_sum(rows):
        send, kept = project(rows, fc_weight, core)
        return kept + along_mp(send, 0, 1).astype(jnp.float32)

    def first_state(summed):
        parts = [
            lax.dynamic_index_in_dim(summed, (x_index + k) % 4, 0, keepdims=False)
            for k in (0, 1, 3, 2)
        ]
        return parts[0] + sum(
            along_mp(part.astype(jnp.bfloat16), k, 0).astype(jnp.float32)
            for part, k in zip(parts[1:], (1, 3, 2))
        )

    own_block = joined_rows
    b01, b10 = step(own_block, 0, 1), step(own_block, 1, 0)
    bm0, b0m = step(own_block, -1, 0), step(own_block, 0, -1)
    round1 = (b0m, b01, bm0, b10)
    next_target = neighbour(target_features[: 2 * PAD], -1)
    next_segments = neighbour(segment_ids[: 2 * PAD], -1)
    last_segments = neighbour(segment_ids[-2 * PAD - 1 :], 1)
    b01, next_target, next_segments, last_segments = barrier(
        (round1[1], next_target, next_segments, last_segments)
    )
    round1 = (round1[0], b01, *round1[2:])
    b0m, b01, bm0, b10 = round1
    bm1, b11 = step(bm0, 0, 1), step(b01, 1, 0)
    bmm, b1m = step(b0m, -1, 0), step(b10, 0, -1)
    round2 = (bmm, bm1, b11, b1m)

    segments = jnp.concatenate([last_segments, segment_ids, next_segments])
    token = mp_index * own - 2 * PAD + jnp.arange(own + 4 * PAD, dtype=jnp.int32)
    keep = (segments[1:] == segments[:-1]) & (token > 0) & (token < total_rows)
    target = jnp.concatenate(
        [jnp.zeros((2 * PAD, columns), jnp.bfloat16), target_features, next_target]
    )
    target = jnp.concatenate(
        [target, jnp.broadcast_to(keep.astype(jnp.bfloat16)[:, None], (target.shape[0], 128))],
        axis=1,
    )
    shares = lax.all_to_all(windows(target, block_rows), "mp", 0, 0, tiled=True)
    round2, shares = barrier((round2, shares))
    shares = shares.reshape(BLOCKS, LENGTH, columns + 128)
    target = shares[..., :columns].astype(jnp.float32)
    keep = shares[..., columns : columns + 1].astype(jnp.float32)
    keep_row = keep.reshape(1, BLOCKS * LENGTH)

    round3 = (step(b0m, 0, -1), step(bm0, -1, 0), step(b11, 1, 0), step(b11, 0, 1))
    early = chip_sum([own_block, *round1, *round2])
    round3, early = barrier((round3, early))
    early = first_state(early)
    b02, b20, b21, b12 = round3
    round4 = (step(bmm, 0, -1), step(bmm, -1, 0), step(b21, 0, 1))
    middle = chip_sum(round3)
    round4, early, middle, target, keep, keep_row = barrier(
        (round4, early, middle, target, keep, keep_row)
    )
    late = first_state(jnp.concatenate([middle, chip_sum(round4)], axis=1))

    names = [
        (0, 0), (0, -1), (0, 1), (-1, 0), (1, 0), (-1, -1), (-1, 1), (1, 1), (1, -1),
        (0, 2), (2, 0), (2, 1), (1, 2), (-1, 2), (2, -1), (2, 2),
    ]
    places = jnp.stack([(y_index + dy) % 4 * 4 + (z_index + dz) % 4 for dy, dz in names])
    places = places.astype(jnp.int32)
    positions = jnp.sum(
        jnp.where(places[None, :] == jnp.arange(BLOCKS)[:, None], jnp.arange(BLOCKS)[None, :], 0),
        axis=1,
    ).astype(jnp.int32)
    states = [early, late]
    before = ring(jnp.concatenate([s[:, SHARE - PAD :] for s in states]), 1)
    after = ring(jnp.concatenate([s[:, :PAD] for s in states]), -1)
    window = assemble(states, before, after, places, mp_index)

    window, positions = barrier((window, positions))
    product = products(window, target, keep, step_gains)
    product = sum_dp(product, AROUND_Z)
    product = [product] + [from_dp(product, place) for place in AROUND_Y]
    low, high = gradients(window, target, keep, keep_row, step_gains, product, factor)

    low1, high3 = along_mp(low, 1, 0), along_mp(high, 3, 0)
    high1, low3 = along_mp(high, 1, 0), along_mp(low, 3, 0)
    low2, high2 = along_mp(low1, 1, 0), along_mp(high3, 3, 0)
    grads = [low, high, low1, high1, low3, high3, low2, high2]
    grads = grads + [along_mp(g, 0, 1) for g in grads]
    owners = [(x_index - k) % 4 * 2 + c for c in (core, 1 - core) for k in (0, 1, 3, 2)]
    grad_weight, mean_loss = weight_gradient(
        [own_block, *round1, *round2, *round3, *round4], positions, grads, owners
    )
    mean_loss = mean_loss[0, 0]
    return (mean_loss, grad_weight)


def solution(mesh):
    in_specs = (P("dp", "mp"), P("mp", "dp"), P("mp", "dp"), P("mp"), P(None, "dp"))
    out_specs = (P(), P("mp", "dp"))
    return jax.shard_map(local, mesh=mesh, in_specs=in_specs, out_specs=out_specs, check_vma=False)
```

```python
import math

import jax
import jax.numpy as jnp
from jax import lax
from jax.experimental import pallas as pl
from jax.experimental.pallas import tpu as pltpu
from jax.sharding import PartitionSpec as P

D = 8192
STEPS = 3
EPSILON = 1e-06

SHARE = 32
PAD = 8
LENGTH = SHARE + 2 * PAD
BLOCKS = 16
PRODUCTS = 24
MIB = 1024 * 1024


def from_dp(block, place):
    route = []
    for y in range(4):
        for z in range(4):
            sy, sz = place(y, z)
            route.append((sy % 4 * 4 + sz % 4, y * 4 + z))
    return lax.ppermute(block, "dp", route)


def along_mp(block, dx, dcore):
    route = [(x * 2 + c, (x + dx) % 4 * 2 + (c ^ dcore)) for x in range(4) for c in range(2)]
    return lax.ppermute(block, "mp", route)


def neighbour(block, distance):
    devices = range(lax.axis_size("mp"))
    route = [(i - distance, i) for i in devices if i - distance in devices]
    return lax.ppermute(block, "mp", route)


def down(block):
    return jnp.concatenate([block[-1:], block[:-1]], axis=0)


def up(block):
    return jnp.concatenate([block[1:], block[:1]], axis=0)


def before(row):
    return jnp.concatenate([row[:, -1:], row[:, :-1]], axis=1)


def after(row):
    return jnp.concatenate([row[:, 1:], row[:, :1]], axis=1)


def tie(value, *others):
    return lax.optimization_barrier((value, *others))[0]


FREE = pl.CostEstimate(flops=1, bytes_accessed=1, transcendentals=0)


def windows_kernel(block_rows, target_ref, out_ref):
    for owner in range(8):
        for block in range(2):
            start = block * block_rows + owner * SHARE + PAD
            out_ref[owner, block] = target_ref[start : start + LENGTH, :]


def windows(target, block_rows):
    return pl.pallas_call(
        lambda *refs: windows_kernel(block_rows, *refs),
        out_shape=jax.ShapeDtypeStruct((8, 2, LENGTH, target.shape[1]), target.dtype),
        in_specs=[pl.BlockSpec(memory_space=pltpu.VMEM)],
        out_specs=pl.BlockSpec(memory_space=pltpu.VMEM),
        compiler_params=pltpu.CompilerParams(vmem_limit_bytes=8 * MIB),
        cost_estimate=FREE,
        name="windows",
    )(target)


def product_kernel(state_ref, target_ref, keep_ref, gain_ref, out_ref, columns):
    gain0, gain1, gain2 = (gain_ref[k : k + 1, :] for k in range(STEPS))
    lane = lax.broadcasted_iota(jnp.int32, (LENGTH, 128), 1)

    def block(index, carry):
        state, target, keep = state_ref[index], target_ref[index], keep_ref[index]
        previous = down(state)
        mixed0 = state + keep * previous
        scaled0 = gain0 * down(mixed0)
        second = gain1 * previous
        third = gain1 * down(scaled0)
        target1 = up(target)
        target2 = gain2 * up(target1)
        weight = gain2 * gain2
        weighted, weighted2, weighted3 = weight * state, weight * second, weight * third
        pairs = [
            (mixed0, mixed0),
            (state, state),
            (state, scaled0),
            (scaled0, scaled0),
            (state, second),
            (state, third),
            (second, second),
            (second, third),
            (third, third),
            (weighted, state),
            (weighted, second),
            (weighted, third),
            (weighted2, second),
            (weighted2, third),
            (weighted3, third),
            (target2, state),
            (target2, second),
            (target2, third),
            (gain1 * target1, state),
            (gain1 * target1, scaled0),
            (gain0 * target, mixed0),
            (target, target),
        ]
        total = jnp.zeros((LENGTH, 128), jnp.float32)
        for k, (left, right) in enumerate(pairs):
            value = jnp.sum(left * right, axis=1, keepdims=True)
            total = jnp.where(lane == k, value, total)
        columns[pl.ds(pl.multiple_of(index * LENGTH, 8), LENGTH), :] = total
        return carry

    lax.fori_loop(0, BLOCKS, block, 0)
    out_ref[...] = columns[...].T[:PRODUCTS, :]


def products(state, target, keep, gains):
    lanes = BLOCKS * LENGTH
    return pl.pallas_call(
        product_kernel,
        out_shape=jax.ShapeDtypeStruct((PRODUCTS, lanes), jnp.float32),
        in_specs=[pl.BlockSpec(memory_space=pltpu.VMEM)] * 4,
        out_specs=pl.BlockSpec(memory_space=pltpu.VMEM),
        scratch_shapes=[pltpu.VMEM((lanes, 128), jnp.float32)],
        compiler_params=pltpu.CompilerParams(vmem_limit_bytes=12 * MIB),
        cost_estimate=FREE,
        name="products",
    )(state, target, keep, gains)


def coefficients(product, keep, factor):
    p = [None] + [product[k : k + 1, :] for k in range(22)]

    def scale(squares):
        return lax.rsqrt(jnp.maximum(squares, 0.0) / D + EPSILON)

    scale0 = scale(p[1])
    r0 = keep * before(scale0)
    scale1 = scale(p[2] + 2.0 * r0 * p[3] + r0 * r0 * p[4])
    a = keep * before(scale1)
    b = a * before(r0)
    scale2 = scale(
        p[2] + a * a * p[7] + b * b * p[9] + 2.0 * a * p[5] + 2.0 * b * p[6] + 2.0 * a * b * p[8]
    )
    same_next = after(keep)
    same_second = same_next * after(same_next)
    x1 = p[10] + a * p[11] + b * p[12]
    x2 = p[11] + a * p[13] + b * p[14]
    x3 = p[12] + a * p[14] + b * p[15]
    product2 = (
        factor
        * same_second
        * scale2
        * (scale2 * (x1 + a * x2 + b * x3) - (p[16] + a * p[17] + b * p[18]))
    )
    alpha2 = factor * same_second * scale2 * scale2
    gamma2 = -factor * same_second * scale2
    beta2 = -scale2 * scale2 * product2 / D
    second = alpha2 * x2 + beta2 * (p[5] + a * p[7] + b * p[8]) + gamma2 * p[17]
    third = alpha2 * x3 + beta2 * (p[6] + a * p[8] + b * p[9]) + gamma2 * p[18]
    next7, next8, next9 = after(p[7]), after(p[8]), after(p[9])
    y1 = next7 + r0 * next8
    y2 = next8 + r0 * next9
    product1 = scale1 * (
        factor * same_next * (scale1 * (y1 + r0 * y2) - (p[19] + r0 * p[20]))
        + same_next * (after(second) + r0 * after(third))
    )
    alpha1 = factor * same_next * scale1 * scale1
    gamma1 = -factor * same_next * scale1
    eta1 = scale1 * same_next
    beta1 = -scale1 * scale1 * product1 / D
    carried = alpha1 * y2 + gamma1 * p[20] + eta1 * after(third) + beta1 * (p[3] + r0 * p[4])
    product0 = scale0 * (
        factor * (scale0 * after(p[4]) - p[21]) + same_next * after(carried)
    )
    alpha0 = factor * scale0 * scale0
    gamma0 = -factor * scale0
    eta0 = scale0 * same_next
    beta0 = -scale0 * scale0 * product0 / D
    goal0 = p[22]
    goal1, goal2 = after(goal0), after(after(goal0))
    squares = (
        scale0 * (scale0 * after(p[4]) - 2.0 * p[21])
        + goal0
        + same_next * (scale1 * (scale1 * (y1 + r0 * y2) - 2.0 * (p[19] + r0 * p[20])) + goal1)
        + same_second
        * (
            scale2 * (scale2 * (x1 + a * x2 + b * x3) - 2.0 * (p[16] + a * p[17] + b * p[18]))
            + goal2
        )
    )
    count = 1.0 + same_next + same_second
    table = [
        r0, a, b, same_next,
        alpha2, beta2, gamma2, alpha1, beta1, gamma1, eta1, alpha0, beta0, gamma0, eta0,
    ]
    return table, squares, count


def gradient_kernel(factor, state_ref, target_ref, keep_ref, keep_row_ref, gain_ref, *refs):
    product_refs, (low_ref, high_ref, table, columns) = refs[:4], refs[4:]
    product = product_refs[0][...]
    for ref in product_refs[1:]:
        product = product + ref[...]
    gain0, gain1, gain2 = (gain_ref[k : k + 1, :] for k in range(STEPS))
    table[...] = jnp.zeros_like(table)
    found, squares, count = coefficients(product, keep_row_ref[...], factor)
    for k, row in enumerate(found):
        table[k : k + 1, :] = row
    columns[...] = table[...].T

    def block(index, grad_ref, first):
        state, target, keep = state_ref[index], target_ref[index], keep_ref[index]
        values = columns[pl.ds(pl.multiple_of(index * LENGTH, 8), LENGTH), :]
        (
            r0, a, b, same_next,
            alpha2, beta2, gamma2, alpha1, beta1, gamma1, eta1, alpha0, beta0, gamma0, eta0,
        ) = (values[:, k : k + 1] for k in range(len(found)))
        previous = down(state)
        mixed0 = state + keep * previous
        scaled0 = gain0 * down(mixed0)
        mixed1 = state + r0 * scaled0
        mixed2 = state + gain1 * (a * previous + b * down(scaled0))
        target1 = up(target)
        target2 = up(target1)
        grad2 = (alpha2 * (gain2 * gain2) + beta2) * mixed2 + gamma2 * (gain2 * target2)
        grad1 = (alpha1 * (gain1 * gain1) + beta1) * mixed1 + gain1 * (
            gamma1 * target1 + eta1 * up(grad2)
        )
        grad0 = (alpha0 * (gain0 * gain0) + beta0) * mixed0 + gain0 * (
            gamma0 * target + eta0 * up(grad1)
        )
        grad = grad0 + grad1 + grad2 + same_next * up(grad0)
        grad_ref[index - first] = grad[PAD : PAD + SHARE].astype(jnp.bfloat16)

    half = BLOCKS // 2
    pl.loop(0, half)(lambda index: block(index, low_ref, 0))
    pl.loop(half, BLOCKS)(lambda index: block(index, high_ref, half))
    place = lax.broadcasted_iota(jnp.int32, squares.shape, 1) % LENGTH
    own_rows = (place >= PAD) & (place < PAD + SHARE)
    parts = []
    for value in (squares, count):
        value = jnp.sum(jnp.where(own_rows, value, 0.0), axis=1, keepdims=True)
        for _ in range(3):
            part = value.astype(jnp.bfloat16).astype(jnp.float32)
            parts.append(part)
            value = value - part
    lane = lax.broadcasted_iota(jnp.int32, high_ref.shape[1:], 1)
    sums = jnp.zeros(lane.shape, jnp.float32)
    for i, part in enumerate(parts):
        sums = jnp.where(lane == i, part, sums)
    high_ref[half] = sums.astype(jnp.bfloat16)


def gradients(state, target, keep, keep_row, gains, product, factor):
    lanes = product[0].shape[1]
    return pl.pallas_call(
        lambda *refs: gradient_kernel(factor, *refs),
        out_shape=tuple(
            jax.ShapeDtypeStruct((BLOCKS // 2 + more, SHARE, state.shape[2]), jnp.bfloat16)
            for more in (0, 1)
        ),
        in_specs=[pl.BlockSpec(memory_space=pltpu.VMEM)] * 9,
        out_specs=(pl.BlockSpec(memory_space=pltpu.VMEM),) * 2,
        scratch_shapes=[
            pltpu.VMEM((128, lanes), jnp.float32),
            pltpu.VMEM((lanes, 128), jnp.float32),
        ],
        compiler_params=pltpu.CompilerParams(vmem_limit_bytes=12 * MIB),
        cost_estimate=FREE,
        name="gradients",
    )(state, target, keep, keep_row, gains, *product)


def project_kernel(pieces, blocks, core_ref, weight_ref, *refs):
    rows, (send_ref, keep_ref, total) = refs[:pieces], refs[pieces:]
    found = jnp.dot(
        jnp.concatenate([r[...] for r in rows], axis=0),
        weight_ref[...],
        preferred_element_type=jnp.float32,
    )

    @pl.when(pl.program_id(0) == 0)
    def _():
        total[...] = found

    @pl.when(pl.program_id(0) == 1)
    def _():
        total[...] += found
        share(blocks, core_ref[0], send_ref, keep_ref, total)


def share(blocks, core, send_ref, keep_ref, total):
    for x in range(4):
        for block in range(blocks):
            start = (block * 4 + x) * 2 * SHARE
            keep = pl.ds(pl.multiple_of(start + core * SHARE, SHARE), SHARE)
            send = pl.ds(pl.multiple_of(start + (1 - core) * SHARE, SHARE), SHARE)
            keep_ref[x, block] = total[keep, :]
            send_ref[x, block] = total[send, :].astype(jnp.bfloat16)


def project(rows, weight, core):
    columns = weight.shape[1]
    tokens = sum(r.shape[0] for r in rows)
    blocks = tokens // (8 * SHARE)
    shape = (4, blocks, SHARE, columns)
    return pl.pallas_call(
        lambda *refs: project_kernel(len(rows), blocks, *refs),
        out_shape=(
            jax.ShapeDtypeStruct(shape, jnp.bfloat16),
            jax.ShapeDtypeStruct(shape, jnp.float32),
        ),
        grid=(2,),
        in_specs=[
            pl.BlockSpec(memory_space=pltpu.SMEM),
            pl.BlockSpec((weight.shape[0] // 2, columns), lambda i: (i, 0)),
        ]
        + [pl.BlockSpec((r.shape[0], r.shape[1] // 2), lambda i: (0, i)) for r in rows],
        out_specs=(pl.BlockSpec(memory_space=pltpu.VMEM),) * 2,
        scratch_shapes=[pltpu.VMEM((tokens, columns), jnp.float32)],
        compiler_params=pltpu.CompilerParams(vmem_limit_bytes=32 * MIB),
        cost_estimate=FREE,
        name="project",
    )(jnp.stack([core]).astype(jnp.int32), weight, *rows)


def assemble_kernel(groups, place_ref, owner_ref, *refs):
    states, (before_ref, after_ref, window_ref) = refs[:groups], refs[groups:]
    first = (owner_ref[0] == 0).astype(jnp.int32)
    last = (owner_ref[0] == 7).astype(jnp.int32)
    edge = jnp.zeros((PAD, window_ref.shape[2]), jnp.float32)
    window_ref[0, :PAD] = edge
    window_ref[BLOCKS - 1, PAD + SHARE :] = edge
    k = 0
    for state_ref in states:
        for i in range(state_ref.shape[0]):
            block = place_ref[k]
            window_ref[block, PAD : PAD + SHARE] = state_ref[i]

            @pl.when(block + first < BLOCKS)
            def _():
                window_ref[jnp.minimum(block + first, BLOCKS - 1), :PAD] = before_ref[k]

            @pl.when(block >= last)
            def _():
                window_ref[jnp.maximum(block - last, 0), PAD + SHARE :] = after_ref[k]

            k += 1


def assemble(states, before, after, places, owner):
    return pl.pallas_call(
        lambda *refs: assemble_kernel(len(states), *refs),
        out_shape=jax.ShapeDtypeStruct((BLOCKS, LENGTH, before.shape[2]), jnp.float32),
        in_specs=[pl.BlockSpec(memory_space=pltpu.SMEM)] * 2
        + [pl.BlockSpec(memory_space=pltpu.VMEM)] * (len(states) + 2),
        out_specs=pl.BlockSpec(memory_space=pltpu.VMEM),
        compiler_params=pltpu.CompilerParams(vmem_limit_bytes=12 * MIB),
        cost_estimate=FREE,
        name="assemble",
    )(places, jnp.stack([owner]).astype(jnp.int32), *states, before, after)


def weight_kernel(pieces, position_ref, owner_ref, *refs):
    rows, grads = refs[:pieces], refs[pieces : pieces + 16]
    out_ref, loss_ref, ordered = refs[pieces + 16 :]
    half = BLOCKS // 2

    @pl.when(pl.program_id(0) == 0)
    def _():
        for i in range(8):
            for block in range(BLOCKS):
                start = (position_ref[block] * 8 + owner_ref[i]) * SHARE
                grad = grads[2 * i + block // half][block % half]
                ordered[pl.ds(pl.multiple_of(start, SHARE), SHARE), :] = grad
        sums = sum(grad_ref[half].astype(jnp.float32) for grad_ref in grads[1::2])
        row = lax.broadcasted_iota(jnp.int32, sums.shape, 0)
        lane = lax.broadcasted_iota(jnp.int32, sums.shape, 1)
        error = jnp.sum(jnp.where((row == 0) & (lane < 3), sums, 0.0))
        count = jnp.sum(jnp.where((row == 0) & (lane >= 3) & (lane < 6), sums, 0.0))
        loss_ref[...] = jnp.full(loss_ref.shape, error / (2.0 * D * count), jnp.float32)

    out_ref[...] = lax.dot_general(
        jnp.concatenate([r[...] for r in rows], axis=0),
        ordered[...],
        (((0,), (0,)), ((), ())),
        preferred_element_type=jnp.float32,
    )


def weight_gradient(rows, positions, grads, owners):
    features, columns = rows[0].shape[1], grads[0].shape[2]
    tokens = sum(r.shape[0] for r in rows)
    width = 512
    return pl.pallas_call(
        lambda *refs: weight_kernel(len(rows), *refs),
        out_shape=(
            jax.ShapeDtypeStruct((features, columns), jnp.float32),
            jax.ShapeDtypeStruct((1, 128), jnp.float32),
        ),
        grid_spec=pltpu.PrefetchScalarGridSpec(
            num_scalar_prefetch=2,
            grid=(features // width,),
            in_specs=[pl.BlockSpec((r.shape[0], width), lambda i, *_: (0, i)) for r in rows]
            + [pl.BlockSpec(g.shape, lambda i, *_: (0, 0, 0)) for g in grads],
            out_specs=(
                pl.BlockSpec((width, columns), lambda i, *_: (i, 0)),
                pl.BlockSpec((1, 128), lambda i, *_: (0, 0)),
            ),
            scratch_shapes=[pltpu.VMEM((tokens, columns), jnp.bfloat16)],
        ),
        compiler_params=pltpu.CompilerParams(vmem_limit_bytes=40 * MIB),
        cost_estimate=FREE,
        name="weight_gradient",
    )(positions, owners, *rows, *grads)


def sum_dp(value, places):
    return value + sum(from_dp(value, place) for place in places)


AROUND_Z = tuple(lambda y, z, k=k: (y, z + k) for k in (1, 3, 2))
AROUND_Y = tuple(lambda y, z, k=k: (y + k, z) for k in (1, 3, 2))


def step(block, dy, dz):
    return from_dp(block, lambda y, z: (y + dy, z + dz))


def ring(block, distance):
    return lax.ppermute(block, "mp", [((i - distance) % 8, i) for i in range(8)])


def local(joined_rows, fc_weight, target_features, segment_ids, step_gains):
    mp_index = lax.axis_index("mp")
    x_index, core = mp_index // 2, mp_index % 2
    dp_index = lax.axis_index("dp")
    y_index, z_index = dp_index // 4, dp_index % 4
    own, columns = target_features.shape
    block_rows = joined_rows.shape[0]
    total_rows = block_rows * lax.axis_size("dp")
    factor = 1.0 / math.sqrt(total_rows)
    barrier = lax.optimization_barrier

    def chip_sum(rows):
        send, kept = project(rows, fc_weight, core)
        return kept + along_mp(send, 0, 1).astype(jnp.float32)

    def first_state(summed):
        parts = [
            lax.dynamic_index_in_dim(summed, (x_index + k) % 4, 0, keepdims=False)
            for k in (0, 1, 3, 2)
        ]
        return parts[0] + sum(
            along_mp(part.astype(jnp.bfloat16), k, 0).astype(jnp.float32)
            for part, k in zip(parts[1:], (1, 3, 2))
        )

    own_block = joined_rows
    b01, b10 = step(own_block, 0, 1), step(own_block, 1, 0)
    bm0, b0m = step(own_block, -1, 0), step(own_block, 0, -1)
    round1 = (b0m, b01, bm0, b10)
    next_target = neighbour(target_features[: 2 * PAD], -1)
    next_segments = neighbour(segment_ids[: 2 * PAD], -1)
    last_segments = neighbour(segment_ids[-2 * PAD - 1 :], 1)
    b01, next_target, next_segments, last_segments = barrier(
        (round1[1], next_target, next_segments, last_segments)
    )
    round1 = (round1[0], b01, *round1[2:])
    b0m, b01, bm0, b10 = round1
    bm1, b11 = step(bm0, 0, 1), step(b01, 1, 0)
    bmm, b1m = step(b0m, -1, 0), step(b10, 0, -1)
    round2 = (bmm, bm1, b11, b1m)

    segments = jnp.concatenate([last_segments, segment_ids, next_segments])
    token = mp_index * own - 2 * PAD + jnp.arange(own + 4 * PAD, dtype=jnp.int32)
    keep = (segments[1:] == segments[:-1]) & (token > 0) & (token < total_rows)
    target = jnp.concatenate(
        [jnp.zeros((2 * PAD, columns), jnp.bfloat16), target_features, next_target]
    )
    target = jnp.concatenate(
        [target, jnp.broadcast_to(keep.astype(jnp.bfloat16)[:, None], (target.shape[0], 128))],
        axis=1,
    )
    shares = lax.all_to_all(windows(target, block_rows), "mp", 0, 0, tiled=True)
    round2, shares = barrier((round2, shares))
    shares = shares.reshape(BLOCKS, LENGTH, columns + 128)
    target = shares[..., :columns].astype(jnp.float32)
    keep = shares[..., columns : columns + 1].astype(jnp.float32)
    keep_row = keep.reshape(1, BLOCKS * LENGTH)

    round3 = (step(b0m, 0, -1), step(bm0, -1, 0), step(b11, 1, 0), step(b11, 0, 1))
    early = chip_sum([own_block, *round1, *round2])
    round3, early = barrier((round3, early))
    early = first_state(early)
    b02, b20, b21, b12 = round3
    round4 = (step(bmm, 0, -1), step(bmm, -1, 0), step(b21, 0, 1))
    middle = chip_sum(round3)
    names = [
        (0, 0), (0, -1), (0, 1), (-1, 0), (1, 0), (-1, -1), (-1, 1), (1, 1), (1, -1),
        (0, 2), (2, 0), (2, 1), (1, 2), (-1, 2), (2, -1), (2, 2),
    ]
    places = jnp.stack([(y_index + dy) % 4 * 4 + (z_index + dz) % 4 for dy, dz in names])
    places = places.astype(jnp.int32)
    positions = jnp.sum(
        jnp.where(places[None, :] == jnp.arange(BLOCKS)[:, None], jnp.arange(BLOCKS)[None, :], 0),
        axis=1,
    ).astype(jnp.int32)
    owners = [(x_index - k) % 4 * 2 + c for c in (core, 1 - core) for k in (0, 1, 3, 2)]
    owners = jnp.stack(owners).astype(jnp.int32)
    round4, early, middle, target, keep, keep_row, places, positions, owners = barrier(
        (round4, early, middle, target, keep, keep_row, places, positions, owners)
    )
    late = first_state(jnp.concatenate([middle, chip_sum(round4)], axis=1))

    states = [early, late]
    before = ring(jnp.concatenate([s[:, SHARE - PAD :] for s in states]), 1)
    after = ring(jnp.concatenate([s[:, :PAD] for s in states]), -1)
    window = assemble(states, before, after, places, mp_index)

    product = products(window, target, keep, step_gains)
    product = sum_dp(product, AROUND_Z)
    product = [product] + [from_dp(product, place) for place in AROUND_Y]
    low, high = gradients(window, target, keep, keep_row, step_gains, product, factor)

    low1, high3 = along_mp(low, 1, 0), along_mp(high, 3, 0)
    high1, low3 = along_mp(high, 1, 0), along_mp(low, 3, 0)
    low2, high2 = along_mp(low1, 1, 0), along_mp(high3, 3, 0)
    grads = [low, high, low1, high1, low3, high3, low2, high2]
    grads = grads + [along_mp(g, 0, 1) for g in grads]
    grad_weight, mean_loss = weight_gradient(
        [own_block, *round1, *round2, *round3, *round4], positions, grads, owners
    )
    mean_loss = mean_loss[0, 0]
    return (mean_loss, grad_weight)


def solution(mesh):
    in_specs = (P("dp", "mp"), P("mp", "dp"), P("mp", "dp"), P("mp"), P(None, "dp"))
    out_specs = (P(), P("mp", "dp"))
    return jax.shard_map(local, mesh=mesh, in_specs=in_specs, out_specs=out_specs, check_vma=False)
```

```python
import math

import jax
import jax.numpy as jnp
from jax import lax
from jax.experimental import pallas as pl
from jax.experimental.pallas import tpu as pltpu
from jax.sharding import PartitionSpec as P

D = 8192
STEPS = 3
EPSILON = 1e-06

SHARE = 32
PAD = 8
LENGTH = SHARE + 2 * PAD
BLOCKS = 16
PRODUCTS = 24
MIB = 1024 * 1024


def from_dp(block, place):
    route = []
    for y in range(4):
        for z in range(4):
            sy, sz = place(y, z)
            route.append((sy % 4 * 4 + sz % 4, y * 4 + z))
    return lax.ppermute(block, "dp", route)


def along_mp(block, dx, dcore):
    route = [(x * 2 + c, (x + dx) % 4 * 2 + (c ^ dcore)) for x in range(4) for c in range(2)]
    return lax.ppermute(block, "mp", route)


def neighbour(block, distance):
    devices = range(lax.axis_size("mp"))
    route = [(i - distance, i) for i in devices if i - distance in devices]
    return lax.ppermute(block, "mp", route)


def down(block):
    return jnp.concatenate([block[-1:], block[:-1]], axis=0)


def up(block):
    return jnp.concatenate([block[1:], block[:1]], axis=0)


def before(row):
    return jnp.concatenate([row[:, -1:], row[:, :-1]], axis=1)


def after(row):
    return jnp.concatenate([row[:, 1:], row[:, :1]], axis=1)


def tie(value, *others):
    return lax.optimization_barrier((value, *others))[0]


FREE = pl.CostEstimate(flops=1, bytes_accessed=1, transcendentals=0)


def windows_kernel(block_rows, target_ref, out_ref):
    for owner in range(8):
        for block in range(2):
            start = block * block_rows + owner * SHARE + PAD
            out_ref[owner, block] = target_ref[start : start + LENGTH, :]


def windows(target, block_rows):
    return pl.pallas_call(
        lambda *refs: windows_kernel(block_rows, *refs),
        out_shape=jax.ShapeDtypeStruct((8, 2, LENGTH, target.shape[1]), target.dtype),
        in_specs=[pl.BlockSpec(memory_space=pltpu.VMEM)],
        out_specs=pl.BlockSpec(memory_space=pltpu.VMEM),
        compiler_params=pltpu.CompilerParams(vmem_limit_bytes=8 * MIB),
        cost_estimate=FREE,
        name="windows",
    )(target)


def product_kernel(state_ref, target_ref, keep_ref, gain_ref, out_ref, columns):
    gain0, gain1, gain2 = (gain_ref[k : k + 1, :] for k in range(STEPS))
    lane = lax.broadcasted_iota(jnp.int32, (LENGTH, 128), 1)

    def block(index, carry):
        state, target, keep = state_ref[index], target_ref[index], keep_ref[index]
        previous = down(state)
        mixed0 = state + keep * previous
        scaled0 = gain0 * down(mixed0)
        second = gain1 * previous
        third = gain1 * down(scaled0)
        target1 = up(target)
        target2 = gain2 * up(target1)
        weight = gain2 * gain2
        weighted, weighted2, weighted3 = weight * state, weight * second, weight * third
        pairs = [
            (mixed0, mixed0),
            (state, state),
            (state, scaled0),
            (scaled0, scaled0),
            (state, second),
            (state, third),
            (second, second),
            (second, third),
            (third, third),
            (weighted, state),
            (weighted, second),
            (weighted, third),
            (weighted2, second),
            (weighted2, third),
            (weighted3, third),
            (target2, state),
            (target2, second),
            (target2, third),
            (gain1 * target1, state),
            (gain1 * target1, scaled0),
            (gain0 * target, mixed0),
            (target, target),
        ]
        total = jnp.zeros((LENGTH, 128), jnp.float32)
        for k, (left, right) in enumerate(pairs):
            value = jnp.sum(left * right, axis=1, keepdims=True)
            total = jnp.where(lane == k, value, total)
        columns[pl.ds(pl.multiple_of(index * LENGTH, 8), LENGTH), :] = total
        return carry

    lax.fori_loop(0, BLOCKS, block, 0, unroll=2)
    out_ref[...] = columns[...].T[:PRODUCTS, :]


def products(state, target, keep, gains):
    lanes = BLOCKS * LENGTH
    return pl.pallas_call(
        product_kernel,
        out_shape=jax.ShapeDtypeStruct((PRODUCTS, lanes), jnp.float32),
        in_specs=[pl.BlockSpec(memory_space=pltpu.VMEM)] * 4,
        out_specs=pl.BlockSpec(memory_space=pltpu.VMEM),
        scratch_shapes=[pltpu.VMEM((lanes, 128), jnp.float32)],
        compiler_params=pltpu.CompilerParams(vmem_limit_bytes=12 * MIB),
        cost_estimate=FREE,
        name="products",
    )(state, target, keep, gains)


def coefficients(product, keep, factor):
    p = [None] + [product[k : k + 1, :] for k in range(22)]

    def scale(squares):
        return lax.rsqrt(jnp.maximum(squares, 0.0) / D + EPSILON)

    scale0 = scale(p[1])
    r0 = keep * before(scale0)
    scale1 = scale(p[2] + 2.0 * r0 * p[3] + r0 * r0 * p[4])
    a = keep * before(scale1)
    b = a * before(r0)
    scale2 = scale(
        p[2] + a * a * p[7] + b * b * p[9] + 2.0 * a * p[5] + 2.0 * b * p[6] + 2.0 * a * b * p[8]
    )
    same_next = after(keep)
    same_second = same_next * after(same_next)
    x1 = p[10] + a * p[11] + b * p[12]
    x2 = p[11] + a * p[13] + b * p[14]
    x3 = p[12] + a * p[14] + b * p[15]
    product2 = (
        factor
        * same_second
        * scale2
        * (scale2 * (x1 + a * x2 + b * x3) - (p[16] + a * p[17] + b * p[18]))
    )
    alpha2 = factor * same_second * scale2 * scale2
    gamma2 = -factor * same_second * scale2
    beta2 = -scale2 * scale2 * product2 / D
    second = alpha2 * x2 + beta2 * (p[5] + a * p[7] + b * p[8]) + gamma2 * p[17]
    third = alpha2 * x3 + beta2 * (p[6] + a * p[8] + b * p[9]) + gamma2 * p[18]
    next7, next8, next9 = after(p[7]), after(p[8]), after(p[9])
    y1 = next7 + r0 * next8
    y2 = next8 + r0 * next9
    product1 = scale1 * (
        factor * same_next * (scale1 * (y1 + r0 * y2) - (p[19] + r0 * p[20]))
        + same_next * (after(second) + r0 * after(third))
    )
    alpha1 = factor * same_next * scale1 * scale1
    gamma1 = -factor * same_next * scale1
    eta1 = scale1 * same_next
    beta1 = -scale1 * scale1 * product1 / D
    carried = alpha1 * y2 + gamma1 * p[20] + eta1 * after(third) + beta1 * (p[3] + r0 * p[4])
    product0 = scale0 * (
        factor * (scale0 * after(p[4]) - p[21]) + same_next * after(carried)
    )
    alpha0 = factor * scale0 * scale0
    gamma0 = -factor * scale0
    eta0 = scale0 * same_next
    beta0 = -scale0 * scale0 * product0 / D
    goal0 = p[22]
    goal1, goal2 = after(goal0), after(after(goal0))
    squares = (
        scale0 * (scale0 * after(p[4]) - 2.0 * p[21])
        + goal0
        + same_next * (scale1 * (scale1 * (y1 + r0 * y2) - 2.0 * (p[19] + r0 * p[20])) + goal1)
        + same_second
        * (
            scale2 * (scale2 * (x1 + a * x2 + b * x3) - 2.0 * (p[16] + a * p[17] + b * p[18]))
            + goal2
        )
    )
    count = 1.0 + same_next + same_second
    table = [
        r0, a, b, same_next,
        alpha2, beta2, gamma2, alpha1, beta1, gamma1, eta1, alpha0, beta0, gamma0, eta0,
    ]
    return table, squares, count


def gradient_kernel(factor, state_ref, target_ref, keep_ref, keep_row_ref, gain_ref, *refs):
    product_refs, (low_ref, high_ref, table, columns) = refs[:4], refs[4:]
    product = product_refs[0][...]
    for ref in product_refs[1:]:
        product = product + ref[...]
    gain0, gain1, gain2 = (gain_ref[k : k + 1, :] for k in range(STEPS))
    table[...] = jnp.zeros_like(table)
    found, squares, count = coefficients(product, keep_row_ref[...], factor)
    for k, row in enumerate(found):
        table[k : k + 1, :] = row
    columns[...] = table[...].T

    def block(index, grad_ref, first):
        state, target, keep = state_ref[index], target_ref[index], keep_ref[index]
        values = columns[pl.ds(pl.multiple_of(index * LENGTH, 8), LENGTH), :]
        (
            r0, a, b, same_next,
            alpha2, beta2, gamma2, alpha1, beta1, gamma1, eta1, alpha0, beta0, gamma0, eta0,
        ) = (values[:, k : k + 1] for k in range(len(found)))
        previous = down(state)
        mixed0 = state + keep * previous
        scaled0 = gain0 * down(mixed0)
        mixed1 = state + r0 * scaled0
        mixed2 = state + gain1 * (a * previous + b * down(scaled0))
        target1 = up(target)
        target2 = up(target1)
        grad2 = (alpha2 * (gain2 * gain2) + beta2) * mixed2 + gamma2 * (gain2 * target2)
        grad1 = (alpha1 * (gain1 * gain1) + beta1) * mixed1 + gain1 * (
            gamma1 * target1 + eta1 * up(grad2)
        )
        grad0 = (alpha0 * (gain0 * gain0) + beta0) * mixed0 + gain0 * (
            gamma0 * target + eta0 * up(grad1)
        )
        grad = grad0 + grad1 + grad2 + same_next * up(grad0)
        grad_ref[index - first] = grad[PAD : PAD + SHARE].astype(jnp.bfloat16)

    half = BLOCKS // 2
    pl.loop(0, half, unroll=2)(lambda index: block(index, low_ref, 0))
    pl.loop(half, BLOCKS, unroll=2)(lambda index: block(index, high_ref, half))
    place = lax.broadcasted_iota(jnp.int32, squares.shape, 1) % LENGTH
    own_rows = (place >= PAD) & (place < PAD + SHARE)
    parts = []
    for value in (squares, count):
        value = jnp.sum(jnp.where(own_rows, value, 0.0), axis=1, keepdims=True)
        for _ in range(3):
            part = value.astype(jnp.bfloat16).astype(jnp.float32)
            parts.append(part)
            value = value - part
    lane = lax.broadcasted_iota(jnp.int32, high_ref.shape[1:], 1)
    sums = jnp.zeros(lane.shape, jnp.float32)
    for i, part in enumerate(parts):
        sums = jnp.where(lane == i, part, sums)
    high_ref[half] = sums.astype(jnp.bfloat16)


def gradients(state, target, keep, keep_row, gains, product, factor):
    lanes = product[0].shape[1]
    return pl.pallas_call(
        lambda *refs: gradient_kernel(factor, *refs),
        out_shape=tuple(
            jax.ShapeDtypeStruct((BLOCKS // 2 + more, SHARE, state.shape[2]), jnp.bfloat16)
            for more in (0, 1)
        ),
        in_specs=[pl.BlockSpec(memory_space=pltpu.VMEM)] * 9,
        out_specs=(pl.BlockSpec(memory_space=pltpu.VMEM),) * 2,
        scratch_shapes=[
            pltpu.VMEM((128, lanes), jnp.float32),
            pltpu.VMEM((lanes, 128), jnp.float32),
        ],
        compiler_params=pltpu.CompilerParams(vmem_limit_bytes=12 * MIB),
        cost_estimate=FREE,
        name="gradients",
    )(state, target, keep, keep_row, gains, *product)


def project_kernel(pieces, blocks, core_ref, weight_ref, *refs):
    rows, (send_ref, keep_ref, total) = refs[:pieces], refs[pieces:]
    found = jnp.dot(
        jnp.concatenate([r[...] for r in rows], axis=0),
        weight_ref[...],
        preferred_element_type=jnp.float32,
    )

    @pl.when(pl.program_id(0) == 0)
    def _():
        total[...] = found

    @pl.when(pl.program_id(0) == 1)
    def _():
        total[...] += found
        share(blocks, core_ref[0], send_ref, keep_ref, total)


def share(blocks, core, send_ref, keep_ref, total):
    for x in range(4):
        for block in range(blocks):
            start = (block * 4 + x) * 2 * SHARE
            keep = pl.ds(pl.multiple_of(start + core * SHARE, SHARE), SHARE)
            send = pl.ds(pl.multiple_of(start + (1 - core) * SHARE, SHARE), SHARE)
            keep_ref[x, block] = total[keep, :]
            send_ref[x, block] = total[send, :].astype(jnp.bfloat16)


def project(rows, weight, core):
    columns = weight.shape[1]
    tokens = sum(r.shape[0] for r in rows)
    blocks = tokens // (8 * SHARE)
    shape = (4, blocks, SHARE, columns)
    return pl.pallas_call(
        lambda *refs: project_kernel(len(rows), blocks, *refs),
        out_shape=(
            jax.ShapeDtypeStruct(shape, jnp.bfloat16),
            jax.ShapeDtypeStruct(shape, jnp.float32),
        ),
        grid=(2,),
        in_specs=[
            pl.BlockSpec(memory_space=pltpu.SMEM),
            pl.BlockSpec((weight.shape[0] // 2, columns), lambda i: (i, 0)),
        ]
        + [pl.BlockSpec((r.shape[0], r.shape[1] // 2), lambda i: (0, i)) for r in rows],
        out_specs=(pl.BlockSpec(memory_space=pltpu.VMEM),) * 2,
        scratch_shapes=[pltpu.VMEM((tokens, columns), jnp.float32)],
        compiler_params=pltpu.CompilerParams(vmem_limit_bytes=32 * MIB),
        cost_estimate=FREE,
        name="project",
    )(jnp.stack([core]).astype(jnp.int32), weight, *rows)


def assemble_kernel(groups, place_ref, owner_ref, *refs):
    states, (before_ref, after_ref, window_ref) = refs[:groups], refs[groups:]
    first = (owner_ref[0] == 0).astype(jnp.int32)
    last = (owner_ref[0] == 7).astype(jnp.int32)
    edge = jnp.zeros((PAD, window_ref.shape[2]), jnp.float32)
    window_ref[0, :PAD] = edge
    window_ref[BLOCKS - 1, PAD + SHARE :] = edge
    k = 0
    for state_ref in states:
        for i in range(state_ref.shape[0]):
            block = place_ref[k]
            window_ref[block, PAD : PAD + SHARE] = state_ref[i]

            @pl.when(block + first < BLOCKS)
            def _():
                window_ref[jnp.minimum(block + first, BLOCKS - 1), :PAD] = before_ref[k]

            @pl.when(block >= last)
            def _():
                window_ref[jnp.maximum(block - last, 0), PAD + SHARE :] = after_ref[k]

            k += 1


def assemble(states, before, after, places, owner):
    return pl.pallas_call(
        lambda *refs: assemble_kernel(len(states), *refs),
        out_shape=jax.ShapeDtypeStruct((BLOCKS, LENGTH, before.shape[2]), jnp.float32),
        in_specs=[pl.BlockSpec(memory_space=pltpu.SMEM)] * 2
        + [pl.BlockSpec(memory_space=pltpu.VMEM)] * (len(states) + 2),
        out_specs=pl.BlockSpec(memory_space=pltpu.VMEM),
        compiler_params=pltpu.CompilerParams(vmem_limit_bytes=12 * MIB),
        cost_estimate=FREE,
        name="assemble",
    )(places, jnp.stack([owner]).astype(jnp.int32), *states, before, after)


def weight_kernel(pieces, position_ref, owner_ref, *refs):
    rows, grads = refs[:pieces], refs[pieces : pieces + 16]
    out_ref, loss_ref, ordered = refs[pieces + 16 :]
    half = BLOCKS // 2

    @pl.when(pl.program_id(0) == 0)
    def _():
        for i in range(8):
            for block in range(BLOCKS):
                start = (position_ref[block] * 8 + owner_ref[i]) * SHARE
                grad = grads[2 * i + block // half][block % half]
                ordered[pl.ds(pl.multiple_of(start, SHARE), SHARE), :] = grad
        sums = sum(grad_ref[half].astype(jnp.float32) for grad_ref in grads[1::2])
        row = lax.broadcasted_iota(jnp.int32, sums.shape, 0)
        lane = lax.broadcasted_iota(jnp.int32, sums.shape, 1)
        error = jnp.sum(jnp.where((row == 0) & (lane < 3), sums, 0.0))
        count = jnp.sum(jnp.where((row == 0) & (lane >= 3) & (lane < 6), sums, 0.0))
        loss_ref[...] = jnp.full(loss_ref.shape, error / (2.0 * D * count), jnp.float32)

    out_ref[...] = lax.dot_general(
        jnp.concatenate([r[...] for r in rows], axis=0),
        ordered[...],
        (((0,), (0,)), ((), ())),
        preferred_element_type=jnp.float32,
    )


def weight_gradient(rows, positions, grads, owners):
    features, columns = rows[0].shape[1], grads[0].shape[2]
    tokens = sum(r.shape[0] for r in rows)
    width = 512
    return pl.pallas_call(
        lambda *refs: weight_kernel(len(rows), *refs),
        out_shape=(
            jax.ShapeDtypeStruct((features, columns), jnp.float32),
            jax.ShapeDtypeStruct((1, 128), jnp.float32),
        ),
        grid_spec=pltpu.PrefetchScalarGridSpec(
            num_scalar_prefetch=2,
            grid=(features // width,),
            in_specs=[pl.BlockSpec((r.shape[0], width), lambda i, *_: (0, i)) for r in rows]
            + [pl.BlockSpec(g.shape, lambda i, *_: (0, 0, 0)) for g in grads],
            out_specs=(
                pl.BlockSpec((width, columns), lambda i, *_: (i, 0)),
                pl.BlockSpec((1, 128), lambda i, *_: (0, 0)),
            ),
            scratch_shapes=[pltpu.VMEM((tokens, columns), jnp.bfloat16)],
        ),
        compiler_params=pltpu.CompilerParams(vmem_limit_bytes=40 * MIB),
        cost_estimate=FREE,
        name="weight_gradient",
    )(positions, owners, *rows, *grads)


def sum_dp(value, places):
    return value + sum(from_dp(value, place) for place in places)


AROUND_Z = tuple(lambda y, z, k=k: (y, z + k) for k in (1, 3, 2))
AROUND_Y = tuple(lambda y, z, k=k: (y + k, z) for k in (1, 3, 2))


def step(block, dy, dz):
    return from_dp(block, lambda y, z: (y + dy, z + dz))


def ring(block, distance):
    return lax.ppermute(block, "mp", [((i - distance) % 8, i) for i in range(8)])


def local(joined_rows, fc_weight, target_features, segment_ids, step_gains):
    mp_index = lax.axis_index("mp")
    x_index, core = mp_index // 2, mp_index % 2
    dp_index = lax.axis_index("dp")
    y_index, z_index = dp_index // 4, dp_index % 4
    own, columns = target_features.shape
    block_rows = joined_rows.shape[0]
    total_rows = block_rows * lax.axis_size("dp")
    factor = 1.0 / math.sqrt(total_rows)
    barrier = lax.optimization_barrier

    def chip_sum(rows):
        send, kept = project(rows, fc_weight, core)
        return kept + along_mp(send, 0, 1).astype(jnp.float32)

    def first_state(summed):
        parts = [
            lax.dynamic_index_in_dim(summed, (x_index + k) % 4, 0, keepdims=False)
            for k in (0, 1, 3, 2)
        ]
        return parts[0] + sum(
            along_mp(part.astype(jnp.bfloat16), k, 0).astype(jnp.float32)
            for part, k in zip(parts[1:], (1, 3, 2))
        )

    own_block = joined_rows
    b01, b10 = step(own_block, 0, 1), step(own_block, 1, 0)
    bm0, b0m = step(own_block, -1, 0), step(own_block, 0, -1)
    round1 = (b0m, b01, bm0, b10)
    next_target = neighbour(target_features[: 2 * PAD], -1)
    next_segments = neighbour(segment_ids[: 2 * PAD], -1)
    last_segments = neighbour(segment_ids[-2 * PAD - 1 :], 1)
    b01, next_target, next_segments, last_segments = barrier(
        (round1[1], next_target, next_segments, last_segments)
    )
    round1 = (round1[0], b01, *round1[2:])
    b0m, b01, bm0, b10 = round1
    bm1, b11 = step(bm0, 0, 1), step(b01, 1, 0)
    bmm, b1m = step(b0m, -1, 0), step(b10, 0, -1)
    round2 = (bmm, bm1, b11, b1m)

    segments = jnp.concatenate([last_segments, segment_ids, next_segments])
    token = mp_index * own - 2 * PAD + jnp.arange(own + 4 * PAD, dtype=jnp.int32)
    keep = (segments[1:] == segments[:-1]) & (token > 0) & (token < total_rows)
    target = jnp.concatenate(
        [jnp.zeros((2 * PAD, columns), jnp.bfloat16), target_features, next_target]
    )
    target = jnp.concatenate(
        [target, jnp.broadcast_to(keep.astype(jnp.bfloat16)[:, None], (target.shape[0], 128))],
        axis=1,
    )
    shares = lax.all_to_all(windows(target, block_rows), "mp", 0, 0, tiled=True)
    round2, shares = barrier((round2, shares))
    shares = shares.reshape(BLOCKS, LENGTH, columns + 128)
    target = shares[..., :columns].astype(jnp.float32)
    keep = shares[..., columns : columns + 1].astype(jnp.float32)
    keep_row = keep.reshape(1, BLOCKS * LENGTH)

    round3 = (step(b0m, 0, -1), step(bm0, -1, 0), step(b11, 1, 0), step(b11, 0, 1))
    early = chip_sum([own_block, *round1, *round2])
    round3, early = barrier((round3, early))
    early = first_state(early)
    b02, b20, b21, b12 = round3
    round4 = (step(bmm, 0, -1), step(bmm, -1, 0), step(b21, 0, 1))
    middle = chip_sum(round3)
    names = [
        (0, 0), (0, -1), (0, 1), (-1, 0), (1, 0), (-1, -1), (-1, 1), (1, 1), (1, -1),
        (0, 2), (2, 0), (2, 1), (1, 2), (-1, 2), (2, -1), (2, 2),
    ]
    places = jnp.stack([(y_index + dy) % 4 * 4 + (z_index + dz) % 4 for dy, dz in names])
    places = places.astype(jnp.int32)
    positions = jnp.sum(
        jnp.where(places[None, :] == jnp.arange(BLOCKS)[:, None], jnp.arange(BLOCKS)[None, :], 0),
        axis=1,
    ).astype(jnp.int32)
    owners = [(x_index - k) % 4 * 2 + c for c in (core, 1 - core) for k in (0, 1, 3, 2)]
    owners = jnp.stack(owners).astype(jnp.int32)
    round4, early, middle, target, keep, keep_row, places, positions, owners = barrier(
        (round4, early, middle, target, keep, keep_row, places, positions, owners)
    )
    late = first_state(jnp.concatenate([middle, chip_sum(round4)], axis=1))

    states = [early, late]
    before = ring(jnp.concatenate([s[:, SHARE - PAD :] for s in states]), 1)
    after = ring(jnp.concatenate([s[:, :PAD] for s in states]), -1)
    window = assemble(states, before, after, places, mp_index)

    product = products(window, target, keep, step_gains)
    product = sum_dp(product, AROUND_Z)
    product = [product] + [from_dp(product, place) for place in AROUND_Y]
    low, high = gradients(window, target, keep, keep_row, step_gains, product, factor)

    low1, high3 = along_mp(low, 1, 0), along_mp(high, 3, 0)
    high1, low3 = along_mp(high, 1, 0), along_mp(low, 3, 0)
    low2, high2 = along_mp(low1, 1, 0), along_mp(high3, 3, 0)
    grads = [low, high, low1, high1, low3, high3, low2, high2]
    grads = grads + [along_mp(g, 0, 1) for g in grads]
    grad_weight, mean_loss = weight_gradient(
        [own_block, *round1, *round2, *round3, *round4], positions, grads, owners
    )
    mean_loss = mean_loss[0, 0]
    return (mean_loss, grad_weight)


def solution(mesh):
    in_specs = (P("dp", "mp"), P("mp", "dp"), P("mp", "dp"), P("mp"), P(None, "dp"))
    out_specs = (P(), P("mp", "dp"))
    return jax.shard_map(local, mesh=mesh, in_specs=in_specs, out_specs=out_specs, check_vma=False)
```

```python
import math

import jax
import jax.numpy as jnp
from jax import lax
from jax.experimental import pallas as pl
from jax.experimental.pallas import tpu as pltpu
from jax.sharding import PartitionSpec as P

D = 8192
STEPS = 3
EPSILON = 1e-06

SHARE = 32
PAD = 8
LENGTH = SHARE + 2 * PAD
BLOCKS = 16
PRODUCTS = 24
MIB = 1024 * 1024


def from_dp(block, place):
    route = []
    for y in range(4):
        for z in range(4):
            sy, sz = place(y, z)
            route.append((sy % 4 * 4 + sz % 4, y * 4 + z))
    return lax.ppermute(block, "dp", route)


def along_mp(block, dx, dcore):
    route = [(x * 2 + c, (x + dx) % 4 * 2 + (c ^ dcore)) for x in range(4) for c in range(2)]
    return lax.ppermute(block, "mp", route)


def neighbour(block, distance):
    devices = range(lax.axis_size("mp"))
    route = [(i - distance, i) for i in devices if i - distance in devices]
    return lax.ppermute(block, "mp", route)


def down(block):
    return jnp.concatenate([block[-1:], block[:-1]], axis=0)


def up(block):
    return jnp.concatenate([block[1:], block[:1]], axis=0)


def before(row):
    return jnp.concatenate([row[:, -1:], row[:, :-1]], axis=1)


def after(row):
    return jnp.concatenate([row[:, 1:], row[:, :1]], axis=1)


def tie(value, *others):
    return lax.optimization_barrier((value, *others))[0]


FREE = pl.CostEstimate(flops=1, bytes_accessed=1, transcendentals=0)


def windows_kernel(block_rows, target_ref, out_ref):
    for owner in range(8):
        for block in range(2):
            start = block * block_rows + owner * SHARE + PAD
            out_ref[owner, block] = target_ref[start : start + LENGTH, :]


def windows(target, block_rows):
    return pl.pallas_call(
        lambda *refs: windows_kernel(block_rows, *refs),
        out_shape=jax.ShapeDtypeStruct((8, 2, LENGTH, target.shape[1]), target.dtype),
        in_specs=[pl.BlockSpec(memory_space=pltpu.VMEM)],
        out_specs=pl.BlockSpec(memory_space=pltpu.VMEM),
        compiler_params=pltpu.CompilerParams(vmem_limit_bytes=8 * MIB),
        cost_estimate=FREE,
        name="windows",
    )(target)


def product_kernel(state_ref, target_ref, keep_ref, gain_ref, out_ref, columns):
    gain0, gain1, gain2 = (gain_ref[k : k + 1, :] for k in range(STEPS))
    lane = lax.broadcasted_iota(jnp.int32, (LENGTH, 128), 1)

    def block(index, carry):
        state, target, keep = state_ref[index], target_ref[index], keep_ref[index]
        previous = down(state)
        mixed0 = state + keep * previous
        scaled0 = gain0 * down(mixed0)
        second = gain1 * previous
        third = gain1 * down(scaled0)
        target1 = up(target)
        target2 = gain2 * up(target1)
        weight = gain2 * gain2
        weighted, weighted2, weighted3 = weight * state, weight * second, weight * third
        pairs = [
            (mixed0, mixed0),
            (state, state),
            (state, scaled0),
            (scaled0, scaled0),
            (state, second),
            (state, third),
            (second, second),
            (second, third),
            (third, third),
            (weighted, state),
            (weighted, second),
            (weighted, third),
            (weighted2, second),
            (weighted2, third),
            (weighted3, third),
            (target2, state),
            (target2, second),
            (target2, third),
            (gain1 * target1, state),
            (gain1 * target1, scaled0),
            (gain0 * target, mixed0),
            (target, target),
        ]
        total = jnp.zeros((LENGTH, 128), jnp.float32)
        for k, (left, right) in enumerate(pairs):
            value = jnp.sum(left * right, axis=1, keepdims=True)
            total = jnp.where(lane == k, value, total)
        columns[pl.ds(pl.multiple_of(index * LENGTH, 8), LENGTH), :] = total
        return carry

    lax.fori_loop(0, BLOCKS, block, 0, unroll=4)
    out_ref[...] = columns[...].T[:PRODUCTS, :]


def products(state, target, keep, gains):
    lanes = BLOCKS * LENGTH
    return pl.pallas_call(
        product_kernel,
        out_shape=jax.ShapeDtypeStruct((PRODUCTS, lanes), jnp.float32),
        in_specs=[pl.BlockSpec(memory_space=pltpu.VMEM)] * 4,
        out_specs=pl.BlockSpec(memory_space=pltpu.VMEM),
        scratch_shapes=[pltpu.VMEM((lanes, 128), jnp.float32)],
        compiler_params=pltpu.CompilerParams(vmem_limit_bytes=12 * MIB),
        cost_estimate=FREE,
        name="products",
    )(state, target, keep, gains)


def coefficients(product, keep, factor):
    p = [None] + [product[k : k + 1, :] for k in range(22)]

    def scale(squares):
        return lax.rsqrt(jnp.maximum(squares, 0.0) / D + EPSILON)

    scale0 = scale(p[1])
    r0 = keep * before(scale0)
    scale1 = scale(p[2] + 2.0 * r0 * p[3] + r0 * r0 * p[4])
    a = keep * before(scale1)
    b = a * before(r0)
    scale2 = scale(
        p[2] + a * a * p[7] + b * b * p[9] + 2.0 * a * p[5] + 2.0 * b * p[6] + 2.0 * a * b * p[8]
    )
    same_next = after(keep)
    same_second = same_next * after(same_next)
    x1 = p[10] + a * p[11] + b * p[12]
    x2 = p[11] + a * p[13] + b * p[14]
    x3 = p[12] + a * p[14] + b * p[15]
    product2 = (
        factor
        * same_second
        * scale2
        * (scale2 * (x1 + a * x2 + b * x3) - (p[16] + a * p[17] + b * p[18]))
    )
    alpha2 = factor * same_second * scale2 * scale2
    gamma2 = -factor * same_second * scale2
    beta2 = -scale2 * scale2 * product2 / D
    second = alpha2 * x2 + beta2 * (p[5] + a * p[7] + b * p[8]) + gamma2 * p[17]
    third = alpha2 * x3 + beta2 * (p[6] + a * p[8] + b * p[9]) + gamma2 * p[18]
    next7, next8, next9 = after(p[7]), after(p[8]), after(p[9])
    y1 = next7 + r0 * next8
    y2 = next8 + r0 * next9
    product1 = scale1 * (
        factor * same_next * (scale1 * (y1 + r0 * y2) - (p[19] + r0 * p[20]))
        + same_next * (after(second) + r0 * after(third))
    )
    alpha1 = factor * same_next * scale1 * scale1
    gamma1 = -factor * same_next * scale1
    eta1 = scale1 * same_next
    beta1 = -scale1 * scale1 * product1 / D
    carried = alpha1 * y2 + gamma1 * p[20] + eta1 * after(third) + beta1 * (p[3] + r0 * p[4])
    product0 = scale0 * (
        factor * (scale0 * after(p[4]) - p[21]) + same_next * after(carried)
    )
    alpha0 = factor * scale0 * scale0
    gamma0 = -factor * scale0
    eta0 = scale0 * same_next
    beta0 = -scale0 * scale0 * product0 / D
    goal0 = p[22]
    goal1, goal2 = after(goal0), after(after(goal0))
    squares = (
        scale0 * (scale0 * after(p[4]) - 2.0 * p[21])
        + goal0
        + same_next * (scale1 * (scale1 * (y1 + r0 * y2) - 2.0 * (p[19] + r0 * p[20])) + goal1)
        + same_second
        * (
            scale2 * (scale2 * (x1 + a * x2 + b * x3) - 2.0 * (p[16] + a * p[17] + b * p[18]))
            + goal2
        )
    )
    count = 1.0 + same_next + same_second
    table = [
        r0, a, b, same_next,
        alpha2, beta2, gamma2, alpha1, beta1, gamma1, eta1, alpha0, beta0, gamma0, eta0,
    ]
    return table, squares, count


def gradient_kernel(factor, state_ref, target_ref, keep_ref, keep_row_ref, gain_ref, *refs):
    product_refs, (low_ref, high_ref, table, columns) = refs[:4], refs[4:]
    product = product_refs[0][...]
    for ref in product_refs[1:]:
        product = product + ref[...]
    gain0, gain1, gain2 = (gain_ref[k : k + 1, :] for k in range(STEPS))
    table[...] = jnp.zeros_like(table)
    found, squares, count = coefficients(product, keep_row_ref[...], factor)
    for k, row in enumerate(found):
        table[k : k + 1, :] = row
    columns[...] = table[...].T

    def block(index, grad_ref, first):
        state, target, keep = state_ref[index], target_ref[index], keep_ref[index]
        values = columns[pl.ds(pl.multiple_of(index * LENGTH, 8), LENGTH), :]
        (
            r0, a, b, same_next,
            alpha2, beta2, gamma2, alpha1, beta1, gamma1, eta1, alpha0, beta0, gamma0, eta0,
        ) = (values[:, k : k + 1] for k in range(len(found)))
        previous = down(state)
        mixed0 = state + keep * previous
        scaled0 = gain0 * down(mixed0)
        mixed1 = state + r0 * scaled0
        mixed2 = state + gain1 * (a * previous + b * down(scaled0))
        target1 = up(target)
        target2 = up(target1)
        grad2 = (alpha2 * (gain2 * gain2) + beta2) * mixed2 + gamma2 * (gain2 * target2)
        grad1 = (alpha1 * (gain1 * gain1) + beta1) * mixed1 + gain1 * (
            gamma1 * target1 + eta1 * up(grad2)
        )
        grad0 = (alpha0 * (gain0 * gain0) + beta0) * mixed0 + gain0 * (
            gamma0 * target + eta0 * up(grad1)
        )
        grad = grad0 + grad1 + grad2 + same_next * up(grad0)
        grad_ref[index - first] = grad[PAD : PAD + SHARE].astype(jnp.bfloat16)

    half = BLOCKS // 2
    pl.loop(0, half, unroll=2)(lambda index: block(index, low_ref, 0))
    pl.loop(half, BLOCKS, unroll=2)(lambda index: block(index, high_ref, half))
    place = lax.broadcasted_iota(jnp.int32, squares.shape, 1) % LENGTH
    own_rows = (place >= PAD) & (place < PAD + SHARE)
    parts = []
    for value in (squares, count):
        value = jnp.sum(jnp.where(own_rows, value, 0.0), axis=1, keepdims=True)
        for _ in range(3):
            part = value.astype(jnp.bfloat16).astype(jnp.float32)
            parts.append(part)
            value = value - part
    lane = lax.broadcasted_iota(jnp.int32, high_ref.shape[1:], 1)
    sums = jnp.zeros(lane.shape, jnp.float32)
    for i, part in enumerate(parts):
        sums = jnp.where(lane == i, part, sums)
    high_ref[half] = sums.astype(jnp.bfloat16)


def gradients(state, target, keep, keep_row, gains, product, factor):
    lanes = product[0].shape[1]
    return pl.pallas_call(
        lambda *refs: gradient_kernel(factor, *refs),
        out_shape=tuple(
            jax.ShapeDtypeStruct((BLOCKS // 2 + more, SHARE, state.shape[2]), jnp.bfloat16)
            for more in (0, 1)
        ),
        in_specs=[pl.BlockSpec(memory_space=pltpu.VMEM)] * 9,
        out_specs=(pl.BlockSpec(memory_space=pltpu.VMEM),) * 2,
        scratch_shapes=[
            pltpu.VMEM((128, lanes), jnp.float32),
            pltpu.VMEM((lanes, 128), jnp.float32),
        ],
        compiler_params=pltpu.CompilerParams(vmem_limit_bytes=12 * MIB),
        cost_estimate=FREE,
        name="gradients",
    )(state, target, keep, keep_row, gains, *product)


def project_kernel(pieces, blocks, core_ref, weight_ref, *refs):
    rows, (send_ref, keep_ref, total) = refs[:pieces], refs[pieces:]
    found = jnp.dot(
        jnp.concatenate([r[...] for r in rows], axis=0),
        weight_ref[...],
        preferred_element_type=jnp.float32,
    )

    @pl.when(pl.program_id(0) == 0)
    def _():
        total[...] = found

    @pl.when(pl.program_id(0) == 1)
    def _():
        total[...] += found
        share(blocks, core_ref[0], send_ref, keep_ref, total)


def share(blocks, core, send_ref, keep_ref, total):
    for x in range(4):
        for block in range(blocks):
            start = (block * 4 + x) * 2 * SHARE
            keep = pl.ds(pl.multiple_of(start + core * SHARE, SHARE), SHARE)
            send = pl.ds(pl.multiple_of(start + (1 - core) * SHARE, SHARE), SHARE)
            keep_ref[x, block] = total[keep, :]
            send_ref[x, block] = total[send, :].astype(jnp.bfloat16)


def project(rows, weight, core):
    columns = weight.shape[1]
    tokens = sum(r.shape[0] for r in rows)
    blocks = tokens // (8 * SHARE)
    shape = (4, blocks, SHARE, columns)
    return pl.pallas_call(
        lambda *refs: project_kernel(len(rows), blocks, *refs),
        out_shape=(
            jax.ShapeDtypeStruct(shape, jnp.bfloat16),
            jax.ShapeDtypeStruct(shape, jnp.float32),
        ),
        grid=(2,),
        in_specs=[
            pl.BlockSpec(memory_space=pltpu.SMEM),
            pl.BlockSpec((weight.shape[0] // 2, columns), lambda i: (i, 0)),
        ]
        + [pl.BlockSpec((r.shape[0], r.shape[1] // 2), lambda i: (0, i)) for r in rows],
        out_specs=(pl.BlockSpec(memory_space=pltpu.VMEM),) * 2,
        scratch_shapes=[pltpu.VMEM((tokens, columns), jnp.float32)],
        compiler_params=pltpu.CompilerParams(vmem_limit_bytes=32 * MIB),
        cost_estimate=FREE,
        name="project",
    )(jnp.stack([core]).astype(jnp.int32), weight, *rows)


def assemble_kernel(groups, place_ref, owner_ref, *refs):
    states, (before_ref, after_ref, window_ref) = refs[:groups], refs[groups:]
    first = (owner_ref[0] == 0).astype(jnp.int32)
    last = (owner_ref[0] == 7).astype(jnp.int32)
    edge = jnp.zeros((PAD, window_ref.shape[2]), jnp.float32)
    window_ref[0, :PAD] = edge
    window_ref[BLOCKS - 1, PAD + SHARE :] = edge
    k = 0
    for state_ref in states:
        for i in range(state_ref.shape[0]):
            block = place_ref[k]
            window_ref[block, PAD : PAD + SHARE] = state_ref[i]

            @pl.when(block + first < BLOCKS)
            def _():
                window_ref[jnp.minimum(block + first, BLOCKS - 1), :PAD] = before_ref[k]

            @pl.when(block >= last)
            def _():
                window_ref[jnp.maximum(block - last, 0), PAD + SHARE :] = after_ref[k]

            k += 1


def assemble(states, before, after, places, owner):
    return pl.pallas_call(
        lambda *refs: assemble_kernel(len(states), *refs),
        out_shape=jax.ShapeDtypeStruct((BLOCKS, LENGTH, before.shape[2]), jnp.float32),
        in_specs=[pl.BlockSpec(memory_space=pltpu.SMEM)] * 2
        + [pl.BlockSpec(memory_space=pltpu.VMEM)] * (len(states) + 2),
        out_specs=pl.BlockSpec(memory_space=pltpu.VMEM),
        compiler_params=pltpu.CompilerParams(vmem_limit_bytes=12 * MIB),
        cost_estimate=FREE,
        name="assemble",
    )(places, jnp.stack([owner]).astype(jnp.int32), *states, before, after)


def weight_kernel(pieces, position_ref, owner_ref, *refs):
    rows, grads = refs[:pieces], refs[pieces : pieces + 16]
    out_ref, loss_ref, ordered = refs[pieces + 16 :]
    half = BLOCKS // 2

    @pl.when(pl.program_id(0) == 0)
    def _():
        for i in range(8):
            for block in range(BLOCKS):
                start = (position_ref[block] * 8 + owner_ref[i]) * SHARE
                grad = grads[2 * i + block // half][block % half]
                ordered[pl.ds(pl.multiple_of(start, SHARE), SHARE), :] = grad
        sums = sum(grad_ref[half].astype(jnp.float32) for grad_ref in grads[1::2])
        row = lax.broadcasted_iota(jnp.int32, sums.shape, 0)
        lane = lax.broadcasted_iota(jnp.int32, sums.shape, 1)
        error = jnp.sum(jnp.where((row == 0) & (lane < 3), sums, 0.0))
        count = jnp.sum(jnp.where((row == 0) & (lane >= 3) & (lane < 6), sums, 0.0))
        loss_ref[...] = jnp.full(loss_ref.shape, error / (2.0 * D * count), jnp.float32)

    out_ref[...] = lax.dot_general(
        jnp.concatenate([r[...] for r in rows], axis=0),
        ordered[...],
        (((0,), (0,)), ((), ())),
        preferred_element_type=jnp.float32,
    )


def weight_gradient(rows, positions, grads, owners):
    features, columns = rows[0].shape[1], grads[0].shape[2]
    tokens = sum(r.shape[0] for r in rows)
    width = 512
    return pl.pallas_call(
        lambda *refs: weight_kernel(len(rows), *refs),
        out_shape=(
            jax.ShapeDtypeStruct((features, columns), jnp.float32),
            jax.ShapeDtypeStruct((1, 128), jnp.float32),
        ),
        grid_spec=pltpu.PrefetchScalarGridSpec(
            num_scalar_prefetch=2,
            grid=(features // width,),
            in_specs=[pl.BlockSpec((r.shape[0], width), lambda i, *_: (0, i)) for r in rows]
            + [pl.BlockSpec(g.shape, lambda i, *_: (0, 0, 0)) for g in grads],
            out_specs=(
                pl.BlockSpec((width, columns), lambda i, *_: (i, 0)),
                pl.BlockSpec((1, 128), lambda i, *_: (0, 0)),
            ),
            scratch_shapes=[pltpu.VMEM((tokens, columns), jnp.bfloat16)],
        ),
        compiler_params=pltpu.CompilerParams(vmem_limit_bytes=40 * MIB),
        cost_estimate=FREE,
        name="weight_gradient",
    )(positions, owners, *rows, *grads)


def sum_dp(value, places):
    return value + sum(from_dp(value, place) for place in places)


AROUND_Z = tuple(lambda y, z, k=k: (y, z + k) for k in (1, 3, 2))
AROUND_Y = tuple(lambda y, z, k=k: (y + k, z) for k in (1, 3, 2))


def step(block, dy, dz):
    return from_dp(block, lambda y, z: (y + dy, z + dz))


def ring(block, distance):
    return lax.ppermute(block, "mp", [((i - distance) % 8, i) for i in range(8)])


def local(joined_rows, fc_weight, target_features, segment_ids, step_gains):
    mp_index = lax.axis_index("mp")
    x_index, core = mp_index // 2, mp_index % 2
    dp_index = lax.axis_index("dp")
    y_index, z_index = dp_index // 4, dp_index % 4
    own, columns = target_features.shape
    block_rows = joined_rows.shape[0]
    total_rows = block_rows * lax.axis_size("dp")
    factor = 1.0 / math.sqrt(total_rows)
    barrier = lax.optimization_barrier

    def chip_sum(rows):
        send, kept = project(rows, fc_weight, core)
        return kept + along_mp(send, 0, 1).astype(jnp.float32)

    def first_state(summed):
        parts = [
            lax.dynamic_index_in_dim(summed, (x_index + k) % 4, 0, keepdims=False)
            for k in (0, 1, 3, 2)
        ]
        return parts[0] + sum(
            along_mp(part.astype(jnp.bfloat16), k, 0).astype(jnp.float32)
            for part, k in zip(parts[1:], (1, 3, 2))
        )

    own_block = joined_rows
    b01, b10 = step(own_block, 0, 1), step(own_block, 1, 0)
    bm0, b0m = step(own_block, -1, 0), step(own_block, 0, -1)
    round1 = (b0m, b01, bm0, b10)
    next_target = neighbour(target_features[: 2 * PAD], -1)
    next_segments = neighbour(segment_ids[: 2 * PAD], -1)
    last_segments = neighbour(segment_ids[-2 * PAD - 1 :], 1)
    b01, next_target, next_segments, last_segments = barrier(
        (round1[1], next_target, next_segments, last_segments)
    )
    round1 = (round1[0], b01, *round1[2:])
    b0m, b01, bm0, b10 = round1
    bm1, b11 = step(bm0, 0, 1), step(b01, 1, 0)
    bmm, b1m = step(b0m, -1, 0), step(b10, 0, -1)
    round2 = (bmm, bm1, b11, b1m)

    segments = jnp.concatenate([last_segments, segment_ids, next_segments])
    token = mp_index * own - 2 * PAD + jnp.arange(own + 4 * PAD, dtype=jnp.int32)
    keep = (segments[1:] == segments[:-1]) & (token > 0) & (token < total_rows)
    target = jnp.concatenate(
        [jnp.zeros((2 * PAD, columns), jnp.bfloat16), target_features, next_target]
    )
    target = jnp.concatenate(
        [target, jnp.broadcast_to(keep.astype(jnp.bfloat16)[:, None], (target.shape[0], 128))],
        axis=1,
    )
    shares = lax.all_to_all(windows(target, block_rows), "mp", 0, 0, tiled=True)
    round2, shares = barrier((round2, shares))
    shares = shares.reshape(BLOCKS, LENGTH, columns + 128)
    target = shares[..., :columns].astype(jnp.float32)
    keep = shares[..., columns : columns + 1].astype(jnp.float32)
    keep_row = keep.reshape(1, BLOCKS * LENGTH)

    round3 = (step(b0m, 0, -1), step(bm0, -1, 0), step(b11, 1, 0), step(b11, 0, 1))
    early = chip_sum([own_block, *round1, *round2])
    round3, early = barrier((round3, early))
    early = first_state(early)
    b02, b20, b21, b12 = round3
    round4 = (step(bmm, 0, -1), step(bmm, -1, 0), step(b21, 0, 1))
    middle = chip_sum(round3)
    names = [
        (0, 0), (0, -1), (0, 1), (-1, 0), (1, 0), (-1, -1), (-1, 1), (1, 1), (1, -1),
        (0, 2), (2, 0), (2, 1), (1, 2), (-1, 2), (2, -1), (2, 2),
    ]
    places = jnp.stack([(y_index + dy) % 4 * 4 + (z_index + dz) % 4 for dy, dz in names])
    places = places.astype(jnp.int32)
    positions = jnp.sum(
        jnp.where(places[None, :] == jnp.arange(BLOCKS)[:, None], jnp.arange(BLOCKS)[None, :], 0),
        axis=1,
    ).astype(jnp.int32)
    owners = [(x_index - k) % 4 * 2 + c for c in (core, 1 - core) for k in (0, 1, 3, 2)]
    owners = jnp.stack(owners).astype(jnp.int32)
    round4, early, middle, target, keep, keep_row, places, positions, owners = barrier(
        (round4, early, middle, target, keep, keep_row, places, positions, owners)
    )
    late = first_state(jnp.concatenate([middle, chip_sum(round4)], axis=1))

    states = [early, late]
    before = ring(jnp.concatenate([s[:, SHARE - PAD :] for s in states]), 1)
    after = ring(jnp.concatenate([s[:, :PAD] for s in states]), -1)
    window = assemble(states, before, after, places, mp_index)

    product = products(window, target, keep, step_gains)
    product = sum_dp(product, AROUND_Z)
    product = [product] + [from_dp(product, place) for place in AROUND_Y]
    low, high = gradients(window, target, keep, keep_row, step_gains, product, factor)

    low1, high3 = along_mp(low, 1, 0), along_mp(high, 3, 0)
    high1, low3 = along_mp(high, 1, 0), along_mp(low, 3, 0)
    low2, high2 = along_mp(low1, 1, 0), along_mp(high3, 3, 0)
    grads = [low, high, low1, high1, low3, high3, low2, high2]
    grads = grads + [along_mp(g, 0, 1) for g in grads]
    grad_weight, mean_loss = weight_gradient(
        [own_block, *round1, *round2, *round3, *round4], positions, grads, owners
    )
    mean_loss = mean_loss[0, 0]
    return (mean_loss, grad_weight)


def solution(mesh):
    in_specs = (P("dp", "mp"), P("mp", "dp"), P("mp", "dp"), P("mp"), P(None, "dp"))
    out_specs = (P(), P("mp", "dp"))
    return jax.shard_map(local, mesh=mesh, in_specs=in_specs, out_specs=out_specs, check_vma=False)
```
